512 devices in a mesh: dp: 32 (over y_hi, x, core), ctx: 16 (over z, y_lo).
Axes of the slice: x: 4, y: 8 (y_hi: 4, y_lo: 2; y = y_hi * 2 + y_lo), z: 8, core: 2. Of those that a mesh axis runs over, the one named last changes fastest.
Arguments:
- hidden_in: bfloat16 [32, 2048, 4096], P('dp', 'ctx'), may hold values from -100 to 100
- query_states: bfloat16 [32, 2048, 256], P('dp', 'ctx'), may hold values from -80 to 80
- key_states: bfloat16 [32, 2048, 128], P('dp', 'ctx'), may hold values from -4 to 4
- value_states: bfloat16 [32, 2048, 128], P('dp', 'ctx'), may hold values from -6 to 6
- out_grad: bfloat16 [32, 2048, 256], P('dp', 'ctx'), may hold values from -6 to 6
- span_order: int32 [32, 32], P('dp'), may hold values from 0 to 31, each once within a row
Outputs:
- clipped_sum: float32 [4096, 512], P('ctx')
The draws below stay inside these ranges and needn't reach their ends.
Inputs may be any that keep to these rules, and one draw needn't show every extreme that they name: Slot s of example e is the stored tokens s * 64 to (s + 1) * 64 - 1; each row of span_order is a permutation of the slots' sequence blocks.
All inputs are finite; a program needn't handle non-finite values.
Results may differ from the reference program's by a relative error of at most 0.0041.
Values may be sent and summed in bfloat16 or wider, within the bound.
A program may use at most 64 MiB of HBM per device.

```python
import math
import jax
import jax.numpy as jnp
from jax import lax

D = 4096
HEAD = 128
QH = 2
TOK_DEV = 128
LENGTH = 2048
COLS = 512
EXAMPLES = 32
N_CTX = 16


def shared_keys(key):
    return jnp.clip(jax.random.normal(key, (EXAMPLES, LENGTH, HEAD), jnp.float32), -4.0, 4.0)


def draw_key_states(key, part):
    drawn = shared_keys(key)
    return drawn.astype(jnp.bfloat16)


def draw_query_states(key, part):
    key = jax.random.fold_in(key, 5)
    random_part = jnp.clip(jax.random.normal(key, (EXAMPLES, LENGTH, QH * HEAD), jnp.float32), -4.0, 4.0)
    return random_part.astype(jnp.bfloat16)


def draw_hidden_in(key, part):
    key = jax.random.fold_in(key, 7)
    feature = jnp.arange(D, dtype=jnp.float32) / D
    random_part = jnp.clip(jax.random.normal(key, (EXAMPLES, LENGTH, D), jnp.float32), -3.0, 3.0)
    column = 10.0 ** feature
    return (random_part * column[None, None, :]).astype(jnp.bfloat16)


def level_of(stream_key, shape, cuts, low, top_value):
    def one(dim, shards_of):
        steps = jax.random.uniform(jax.random.fold_in(jax.random.fold_in(stream_key, 6), dim), (shards_of,), jnp.float32, low / len(cuts), top_value / len(cuts))
        return jnp.repeat(jnp.exp(steps), shape[dim] // shards_of).reshape((-1,) + (1,) * (len(shape) - dim - 1))

    factor_of = one(*cuts[0])
    for cut in cuts[1:]:
        factor_of = factor_of * one(*cut)
    return factor_of


def noise(own_key, extent, scale, most, cuts=(), kind=jnp.bfloat16):
    loudness = level_of(own_key, extent, cuts, -0.22, 0.18) if cuts else 1.0
    values = jax.random.normal(own_key, extent, jnp.float32) * scale * loudness
    return jnp.minimum(jnp.maximum(values, -most), most).astype(kind)


def setup_inputs(seed: int = 0) -> dict:
    arg_keys = jax.random.split(jax.random.key(seed), 7)
    return {
        "hidden_in": draw_hidden_in(jax.random.fold_in(arg_keys[6], 71), 0),
        "query_states": draw_query_states(jax.random.fold_in(arg_keys[6], 71), 0),
        "key_states": draw_key_states(jax.random.fold_in(arg_keys[6], 71), 0),
        "value_states": noise(arg_keys[3], (EXAMPLES, LENGTH, HEAD), 1.0, 6.0, ((0, 32), (1, 16))),
        "out_grad": noise(arg_keys[4], (EXAMPLES, LENGTH, QH * HEAD), 1.0, 6.0, ((0, 32), (1, 16))),
        "span_order": jax.vmap(lambda own: jax.random.permutation(own, 2 * N_CTX))(jax.random.split(arg_keys[5], EXAMPLES)).reshape((EXAMPLES, 2 * N_CTX)).astype(jnp.int32),
    }


masked_fill = -1e+30
gamma_floor = 0.01

def token_positions(span_table):
    span_len = TOK_DEV // 2
    row_ids = jnp.arange(LENGTH, dtype=jnp.int32)
    return span_table[row_ids // span_len].astype(jnp.int32) * span_len + row_ids % span_len

def example_grad(hidden, queries, key_rows, value_rows, grad_out, span_table):
    positions = token_positions(span_table)
    allowed = positions[None, :] <= positions[:, None]
    inv_scale = 1.0 / math.sqrt(HEAD)
    query_parts = []
    key_acc = jnp.zeros((LENGTH, HEAD), jnp.float32)
    value_acc = jnp.zeros((LENGTH, HEAD), jnp.float32)
    for head_idx in range(QH):
        query_head = queries[:, head_idx * HEAD:(head_idx + 1) * HEAD]
        grad_head = grad_out[:, head_idx * HEAD:(head_idx + 1) * HEAD]
        raw = jnp.dot(query_head, key_rows.T, preferred_element_type=jnp.float32) * inv_scale
        scores = jnp.where(allowed, raw, masked_fill)
        row_max = lax.optimization_barrier(jnp.max(scores, axis=1, keepdims=True))
        log_total = row_max + jnp.log(lax.optimization_barrier(jnp.sum(jnp.exp(scores - row_max), axis=1, keepdims=True)))
        weights = jnp.where(allowed, jnp.exp(scores - log_total), 0.0)
        grad_probs = jnp.dot(grad_head, value_rows.T, preferred_element_type=jnp.float32)
        row_delta = lax.optimization_barrier(jnp.sum(weights * grad_probs, axis=1, keepdims=True))
        grad_scores = weights * (grad_probs - row_delta)
        weights_low = weights.astype(jnp.bfloat16)
        scores_low = grad_scores.astype(jnp.bfloat16)
        query_grad = jnp.dot(scores_low, key_rows, preferred_element_type=jnp.float32) * inv_scale
        query_parts.append(query_grad.astype(jnp.bfloat16))
        key_acc = key_acc + jnp.dot(scores_low.T, query_head, preferred_element_type=jnp.float32) * inv_scale
        value_acc = value_acc + jnp.dot(weights_low.T, grad_head, preferred_element_type=jnp.float32)
    grads = jnp.concatenate(query_parts + [key_acc.astype(jnp.bfloat16), value_acc.astype(jnp.bfloat16)], axis=1)
    full_grad = jnp.dot(hidden.T, grads, preferred_element_type=jnp.float32)
    norm_sq = jnp.sum(full_grad * full_grad)
    return full_grad * (math.sqrt(D * COLS / EXAMPLES) / (jnp.sqrt(norm_sq) + gamma_floor))

def reference(hidden_in, query_states, key_states, value_states, out_grad, span_order):

    def accumulate(running, example):
        hidden, queries, key_rows, value_rows, grad_out, span_table = example
        return (running + example_grad(hidden, queries, key_rows, value_rows, grad_out, span_table), None)
    start_sum = jnp.zeros((D, COLS), jnp.float32)
    running, unused = lax.scan(accumulate, start_sum, (hidden_in, query_states, key_states, value_states, out_grad, span_order))
    return running
```

```python
import functools
import math

import jax
import jax.numpy as jnp
from jax import lax
from jax.experimental import pallas as pl
from jax.experimental.pallas import tpu as pltpu
from jax.sharding import PartitionSpec as P

MESH = pl.DeviceIdType.MESH
F32 = jnp.float32
BF16 = jnp.bfloat16

masked_fill = -1e30
gamma_floor = 0.01

TOK = 128
HEAD = 128
SPAN = 64
NZ = 8
FEAT = 256
COLS = 512
CHIPS = 16


def aligned(index, size):
    return pl.ds(pl.multiple_of(index * size, size), size)


def contract(left, right, left_dim, right_dim):
    return lax.dot_general(
        left, right, (((left_dim,), (right_dim,)), ((), ())), preferred_element_type=F32
    )


def kernel(
    scale_total,
    h_ref,
    q_ref,
    k_ref,
    v_ref,
    do_ref,
    span_ref,
    out_ref,
    hid,
    kv,
    qd,
    qs,
    stat_out,
    stat_in,
    expo,
    dprob,
    low_s,
    part_out,
    part_in,
    dq_out,
    dq_in,
    grads,
    acc,
    norm_box,
    half_in,
    fac_out,
    fac_in,
    rs_out,
    rs_in,
    ag,
    ag_far,
    hid_ss,
    hid_rs,
    ring_ss,
    ring_rs,
    pair_ss,
    pair_rs,
    fwd_ss,
    fwd_rs,
    part_ss,
    part_rs,
    norm_ss,
    norm_rs,
    rs_ss,
    rs_rs,
    ag_ss,
    ag_rs,
    own_sem,
):
    dp = lax.axis_index("dp")
    ctx = lax.axis_index("ctx")
    z = ctx // 2
    yl = lax.rem(ctx, 2)
    core = lax.rem(dp, 2)
    chip = dp // 2
    inv_scale = 1.0 / math.sqrt(HEAD)

    def zed(step):
        return lax.rem(z + step + NZ, NZ)

    up = (dp, zed(1) * 2 + yl)
    down = (dp, zed(-1) * 2 + yl)
    pair = (dp, z * 2 + (1 - yl))
    twin = (chip * 2 + (1 - core), ctx)

    def send(src, dst, ss, rs, device):
        copy = pltpu.make_async_remote_copy(
            src_ref=src, dst_ref=dst, send_sem=ss, recv_sem=rs,
            device_id=device, device_id_type=MESH,
        )
        copy.start()
        return copy

    barrier = pltpu.get_barrier_semaphore()
    for step in range(1, 16):
        pl.semaphore_signal(
            barrier, inc=1, device_id=(dp, lax.rem(ctx + step, 16)), device_id_type=MESH
        )
    for step in range(1, CHIPS):
        other = lax.rem(chip + step, CHIPS) * 2 + core
        pl.semaphore_signal(barrier, inc=1, device_id=(other, ctx), device_id_type=MESH)
    pl.semaphore_signal(barrier, inc=1, device_id=twin, device_id_type=MESH)

    kv[z, :, :HEAD] = k_ref[0]
    kv[z, :, HEAD:] = v_ref[0]
    qd[yl, :, : 2 * HEAD] = q_ref[0]
    qd[yl, :, 2 * HEAD :] = do_ref[0]
    pl.semaphore_wait(barrier, 31)

    started = []

    qd_copy = send(qd.at[yl], qd.at[yl], pair_ss.at[0], pair_rs.at[0], pair)

    def ring_send(lane, step, view_up, view_down):
        first = send(view_up, view_up, ring_ss.at[lane, 0, step], ring_rs.at[lane, 0, step], up)
        second = send(
            view_down, view_down, ring_ss.at[lane, 1, step], ring_rs.at[lane, 1, step], down
        )
        started.extend([first, second])
        return first, second

    def kv_views(step):
        if step < 4:
            return kv.at[zed(1 - step)], kv.at[zed(step - 1)]
        return kv.at[zed(-3), :, :HEAD], kv.at[zed(3), :, HEAD:]

    kv_copies = ring_send(0, 1, *kv_views(1))

    own_copy = pltpu.make_async_copy(
        h_ref.at[0, :, aligned(ctx, FEAT)], hid.at[z, aligned(yl, TOK), :], own_sem
    )
    own_copy.start()

    lane = lax.broadcasted_iota(jnp.int32, (1, 4 * HEAD), 1)
    token = lax.rem(lane, 2 * TOK)
    slot = token // SPAN
    first_slot = z * 4
    query_pos = jnp.full((1, 4 * HEAD), 0, jnp.int32)
    for s in range(4):
        query_pos = jnp.where(slot == s, span_ref[0, first_slot + s], query_pos)
    query_pos = query_pos * SPAN + lax.rem(token, SPAN)
    row = lax.broadcasted_iota(jnp.int32, (TOK, 4 * HEAD), 0)
    row_low = row < SPAN

    qd_copy.wait()
    for h in range(2):
        for y in range(2):
            rows = pl.ds(h * 2 * TOK + y * TOK, TOK)
            qs[0, rows, :] = qd[y, :, h * HEAD : (h + 1) * HEAD]
            qs[1, rows, :] = qd[y, :, (2 + h) * HEAD : (3 + h) * HEAD]

    tops, sums, dots = [], [], []

    def first_pass(place, block_z):
        keys = kv[block_z, :, :HEAD]
        values = kv[block_z, :, HEAD:]
        key_slot = (block_z * 2 + yl) * 2
        low = span_ref[0, key_slot] * SPAN
        high = span_ref[0, key_slot + 1] * SPAN - SPAN
        key_pos = jnp.where(row_low, low, high) + row
        raw = contract(keys, qs[0], 1, 1) * inv_scale
        scores = jnp.where(key_pos <= query_pos, raw, masked_fill)
        probs = contract(values, qs[1], 1, 1)
        top = jnp.max(scores, axis=0, keepdims=True)
        weights = jnp.exp(scores - top)
        expo[place] = weights
        dprob[place] = probs
        tops.append(top)
        sums.append(jnp.sum(weights, axis=0, keepdims=True))
        dots.append(jnp.sum(weights * probs, axis=0, keepdims=True))

    order = [0]
    first_pass(0, z)
    for step in range(1, 5):
        for copy in kv_copies:
            copy.wait_recv()
        if step < 4:
            kv_copies = ring_send(0, step + 1, *kv_views(step + 1))
            order += [-step, step]
            first_pass(2 * step - 1, zed(-step))
            first_pass(2 * step, zed(step))
        else:
            order += [4]
            first_pass(7, zed(4))

    hid_copies = []
    for step in [8, 9, 7, 10, 6, 11, 5, 12, 4, 13, 3, 14, 2, 15, 1]:
        peer = lax.rem(ctx + step, 16)
        hid_copies.append(
            send(
                h_ref.at[0, :, aligned(peer, FEAT)],
                hid.at[z, aligned(yl, TOK), :],
                hid_ss.at[step], hid_rs.at[step], (dp, peer),
            )
        )

    started.extend(hid_copies)

    top = functools.reduce(jnp.maximum, tops)
    total = sum(jnp.exp(t - top) * s for t, s in zip(tops, sums))
    dot = sum(jnp.exp(t - top) * d for t, d in zip(tops, dots))
    stat_out[...] = jnp.concatenate([top, total, dot] + [top] * 5, axis=0)
    send(stat_out, stat_in, pair_ss.at[1], pair_rs.at[1], pair).wait()
    far_top = stat_in[0:1, :]
    whole_top = jnp.maximum(top, far_top)
    mine, far = jnp.exp(top - whole_top), jnp.exp(far_top - whole_top)
    whole_sum = mine * total + far * stat_in[1:2, :]
    log_total = whole_top + jnp.log(whole_sum)
    row_delta = (mine * dot + far * stat_in[2:3, :]) / whole_sum

    part_copies = []
    own_part = None
    for place in [7, 5, 6, 3, 4, 1, 2, 0]:
        shift = order[place]
        probs = expo[place] * jnp.exp(tops[place] - log_total)
        scores_low = (probs * (dprob[place] - row_delta)).astype(BF16)
        low_s[place] = scores_low
        key_add = jnp.dot(scores_low, qs[0], preferred_element_type=F32) * inv_scale
        value_add = jnp.dot(probs.astype(BF16), qs[1], preferred_element_type=F32)
        if shift == 0:
            own_part = (key_add, value_add)
            continue
        part_out[place, :, :HEAD] = key_add.astype(BF16)
        part_out[place, :, HEAD:] = value_add.astype(BF16)
        part_copies.append(
            send(
                part_out.at[place], part_in.at[place],
                part_ss.at[place], part_rs.at[place], (dp, zed(shift) * 2 + yl),
            )
        )

    query_sum = jnp.zeros((HEAD, 4 * HEAD), F32)
    for place in range(8):
        query_sum += contract(kv[zed(order[place]), :, :HEAD], low_s[place], 0, 0)
    query_sum = query_sum.T * inv_scale
    acc[:, :HEAD] = query_sum[: 2 * TOK]
    acc[:, HEAD : 2 * HEAD] = query_sum[2 * TOK :]
    dq_out[...] = acc[aligned(1 - yl, TOK), : 2 * HEAD].astype(BF16)
    send(dq_out, dq_in, pair_ss.at[2], pair_rs.at[2], pair).wait()
    query_grad = acc[aligned(yl, TOK), : 2 * HEAD] + dq_in[...].astype(F32)
    grads[z, aligned(yl, TOK), : 2 * HEAD] = query_grad.astype(BF16)

    mine_rows = aligned(yl, TOK)

    def forward(lane, place, block_z, columns):
        view = grads.at[block_z, mine_rows, columns]
        copy = send(view, view, fwd_ss.at[lane, place], fwd_rs.at[lane, place], pair)
        started.append(copy)
        return copy

    def z_first(lane, start, width):
        half = width // 2

        def views(step):
            if step < 4:
                return (
                    grads.at[zed(1 - step), mine_rows, pl.ds(start, width)],
                    grads.at[zed(step - 1), mine_rows, pl.ds(start, width)],
                )
            if half >= 128:
                return (
                    grads.at[zed(-3), mine_rows, pl.ds(start, half)],
                    grads.at[zed(3), mine_rows, pl.ds(start + half, half)],
                )
            low = pl.ds(pl.multiple_of(yl * TOK, 64), TOK // 2)
            high = pl.ds(pl.multiple_of(yl * TOK + TOK // 2, 64), TOK // 2)
            return (
                grads.at[zed(-3), low, pl.ds(start, width)],
                grads.at[zed(3), high, pl.ds(start, width)],
            )

        columns = pl.ds(start, width)
        arrivals = [forward(lane, 0, z, columns)]
        copies = ring_send(lane, 1, *views(1))
        for step in range(1, 5):
            for copy in copies:
                copy.wait_recv()
            if step < 4:
                copies = ring_send(lane, step + 1, *views(step + 1))
                arrivals.append(forward(lane, 2 * step - 1, zed(-step), columns))
                arrivals.append(forward(lane, 2 * step, zed(step), columns))
            else:
                arrivals.append(forward(lane, 7, zed(4), columns))
            yield None
        yield arrivals

    def y_first(lane, start, width):
        columns = pl.ds(start, width)
        exchange = forward(lane, 0, z, columns)

        def views(step):
            if step < 4:
                return (
                    grads.at[zed(1 - step), :, columns],
                    grads.at[zed(step - 1), :, columns],
                )
            return (
                grads.at[zed(-3), pl.ds(0, TOK), columns],
                grads.at[zed(3), pl.ds(TOK, TOK), columns],
            )

        exchange.wait_recv()
        copies = ring_send(lane, 1, *views(1))
        for step in range(1, 5):
            for copy in copies:
                copy.wait_recv()
            if step < 4:
                copies = ring_send(lane, step + 1, *views(step + 1))
            yield None
        yield []

    query_arrivals = list(z_first(1, 0, 2 * HEAD))[-1]

    key_sum, value_sum = own_part
    for copy in part_copies:
        copy.wait_recv()
    for place in range(1, 8):
        key_sum = key_sum + part_in[place, :, :HEAD].astype(F32)
        value_sum = value_sum + part_in[place, :, HEAD:].astype(F32)
    grads[z, mine_rows, pl.ds(2 * HEAD, HEAD)] = key_sum.astype(BF16)
    grads[z, mine_rows, pl.ds(3 * HEAD, HEAD)] = value_sum.astype(BF16)

    value_lane = z_first(2, 3 * HEAD, HEAD)
    key_lane = y_first(3, 2 * HEAD, HEAD)
    arrivals = []
    for _ in range(5):
        arrivals = next(value_lane)
        next(key_lane)
    for copy in query_arrivals + arrivals:
        copy.wait_recv()
    own_copy.wait()
    for copy in hid_copies:
        copy.wait_recv()

    for block in range(NZ):
        part = contract(hid[block], grads[block], 0, 0)
        if block == 0:
            acc[...] = part
        else:
            acc[...] += part

    near_rows = aligned(core, TOK)
    half_copy = send(
        acc.at[aligned(1 - core, TOK)], half_in, pair_ss.at[3], pair_rs.at[3], twin
    )
    whole = acc[...]
    squares = jnp.sum((whole * whole).reshape(32, 8, COLS), axis=0)
    tile = squares[:, :128] + squares[:, 128:256] + squares[:, 256:384] + squares[:, 384:]
    norm_box[ctx] = tile
    norm_copies = []
    for step in range(1, 16):
        norm_copies.append(
            send(
                norm_box.at[ctx], norm_box.at[ctx], norm_ss.at[step], norm_rs.at[step],
                (dp, lax.rem(ctx + step, 16)),
            )
        )
    for copy in norm_copies:
        copy.wait()
    total_sq = jnp.sum(jnp.sum(norm_box[...], axis=0), axis=(0, 1), keepdims=True)
    factor = scale_total / (jnp.sqrt(total_sq) + gamma_floor)
    factor = jnp.broadcast_to(factor, (8, 128))
    fac_out[...] = factor
    send(fac_out, fac_in, pair_ss.at[4], pair_rs.at[4], twin).wait()
    half_copy.wait()
    mixed = acc[near_rows, :] * factor[0:1, 0:1] + half_in[...] * fac_in[0:1, 0:1]
    for place in range(CHIPS):
        r, w = (place % 8) * 16, (place // 8) * FEAT
        rs_out[place] = mixed[r : r + 16, w : w + FEAT].astype(BF16)
    rs_copies = []
    for step in range(1, CHIPS):
        other = lax.rem(chip + step, CHIPS)
        rs_copies.append(
            send(
                rs_out.at[other], rs_in.at[chip], rs_ss.at[step], rs_rs.at[step],
                (other * 2 + core, ctx),
            )
        )
    rs_in[chip] = rs_out[chip]
    for copy in rs_copies:
        copy.wait()
    piece = rs_in[0].astype(F32)
    for place in range(1, CHIPS):
        piece = piece + rs_in[place].astype(F32)
    ag[chip] = piece.astype(BF16)
    ag_copies = []
    for step in range(1, CHIPS):
        other = lax.rem(chip + step, CHIPS)
        ag_copies.append(
            send(
                ag.at[chip], ag.at[chip], ag_ss.at[step], ag_rs.at[step],
                (other * 2 + core, ctx),
            )
        )
    for copy in ag_copies:
        copy.wait()
    last = send(ag, ag_far, pair_ss.at[5], pair_rs.at[5], twin)
    for place in range(CHIPS):
        r, w = (place % 8) * 16, (place // 8) * FEAT
        rows = pl.ds(pl.multiple_of(core * TOK + r, 16), 16)
        out_ref[rows, pl.ds(w, FEAT)] = ag[place].astype(F32)
    last.wait()
    for place in range(CHIPS):
        r, w = (place % 8) * 16, (place // 8) * FEAT
        rows = pl.ds(pl.multiple_of((1 - core) * TOK + r, 16), 16)
        out_ref[rows, pl.ds(w, FEAT)] = ag_far[place].astype(F32)
    for copy in started + part_copies:
        copy.wait_send()


def on_device(hidden_in, query_states, key_states, value_states, out_grad, span_order):
    scale_total = math.sqrt(hidden_in.shape[2] * COLS / lax.axis_size("dp"))
    vmem = pl.BlockSpec(memory_space=pltpu.VMEM)
    dma = pltpu.SemaphoreType.DMA
    return pl.pallas_call(
        functools.partial(kernel, scale_total),
        name="clipped_grads",
        out_shape=jax.ShapeDtypeStruct((FEAT, COLS), F32),
        in_specs=[
            pl.BlockSpec(memory_space=pl.ANY), vmem, vmem, vmem, vmem,
            pl.BlockSpec(memory_space=pltpu.SMEM),
        ],
        out_specs=vmem,
        scratch_shapes=[
            pltpu.VMEM((NZ, 2 * TOK, FEAT), BF16),
            pltpu.VMEM((NZ, TOK, 2 * HEAD), BF16),
            pltpu.VMEM((2, TOK, 4 * HEAD), BF16),
            pltpu.VMEM((2, 4 * TOK, HEAD), BF16),
            pltpu.VMEM((8, 4 * HEAD), F32),
            pltpu.VMEM((8, 4 * HEAD), F32),
            pltpu.VMEM((NZ, TOK, 4 * HEAD), F32),
            pltpu.VMEM((NZ, TOK, 4 * HEAD), F32),
            pltpu.VMEM((NZ, TOK, 4 * HEAD), BF16),
            pltpu.VMEM((NZ, TOK, 2 * HEAD), BF16),
            pltpu.VMEM((NZ, TOK, 2 * HEAD), BF16),
            pltpu.VMEM((TOK, 2 * HEAD), BF16),
            pltpu.VMEM((TOK, 2 * HEAD), BF16),
            pltpu.VMEM((NZ, 2 * TOK, COLS), BF16),
            pltpu.VMEM((FEAT, COLS), F32),
            pltpu.VMEM((16, 8, 128), F32),
            pltpu.VMEM((TOK, COLS), F32),
            pltpu.VMEM((8, 128), F32),
            pltpu.VMEM((8, 128), F32),
            pltpu.VMEM((CHIPS, 16, FEAT), BF16),
            pltpu.VMEM((CHIPS, 16, FEAT), BF16),
            pltpu.VMEM((CHIPS, 16, FEAT), BF16),
            pltpu.VMEM((CHIPS, 16, FEAT), BF16),
            dma((16,)), dma((16,)),
            dma((4, 2, 5)), dma((4, 2, 5)),
            dma((6,)), dma((6,)),
            dma((4, 8)), dma((4, 8)),
            dma((8,)), dma((8,)),
            dma((16,)), dma((16,)),
            dma((16,)), dma((16,)),
            dma((16,)), dma((16,)),
            dma,
        ],
        compiler_params=pltpu.CompilerParams(
            collective_id=0, has_side_effects=True, vmem_limit_bytes=48 << 20
        ),
    )(hidden_in, query_states, key_states, value_states, out_grad, span_order)


def solution(mesh):
    return jax.shard_map(
        on_device,
        mesh=mesh,
        in_specs=(
            P("dp", "ctx", None),
            P("dp", "ctx", None),
            P("dp", "ctx", None),
            P("dp", "ctx", None),
            P("dp", "ctx", None),
            P("dp", None),
        ),
        out_specs=P("ctx", None),
        check_vma=False,
    )
```

```python
import functools
import math

import jax
import jax.numpy as jnp
from jax import lax
from jax.experimental import pallas as pl
from jax.experimental.pallas import tpu as pltpu
from jax.sharding import PartitionSpec as P

MESH = pl.DeviceIdType.MESH
F32 = jnp.float32
BF16 = jnp.bfloat16

masked_fill = -1e30
gamma_floor = 0.01

TOK = 128
HEAD = 128
SPAN = 64
NZ = 8
FEAT = 256
COLS = 512
CHIPS = 16


def aligned(index, size):
    return pl.ds(pl.multiple_of(index * size, size), size)


def contract(left, right, left_dim, right_dim):
    return lax.dot_general(
        left, right, (((left_dim,), (right_dim,)), ((), ())), preferred_element_type=F32
    )


class Sent:
    def __init__(self, copy):
        self.copy = copy
        self.open_send = self.open_recv = True
        copy.start()

    def wait_recv(self):
        if self.open_recv:
            self.copy.wait_recv()
        self.open_recv = False

    def wait_send(self):
        if self.open_send:
            self.copy.wait_send()
        self.open_send = False


def kernel(
    scale_total,
    h_ref,
    q_ref,
    k_ref,
    v_ref,
    do_ref,
    span_ref,
    out_ref,
    hid,
    raw,
    keys,
    keys_t,
    values,
    queries,
    douts,
    expo,
    dprob,
    tops,
    key_acc,
    value_acc,
    grads,
    acc,
    norm_box,
    norm_far,
    half_in,
    rs_out,
    rs_in,
    ag,
    ag_far,
    spans,
    slots,
    hid_ss,
    hid_rs,
    ring_ss,
    ring_rs,
    twin_ss,
    twin_rs,
    fwd_ss,
    fwd_rs,
    norm_ss,
    norm_rs,
    rs_ss,
    rs_rs,
    ag_ss,
    ag_rs,
    own_sem,
):
    dp = lax.axis_index("dp")
    ctx = lax.axis_index("ctx")
    z = ctx // 2
    yl = lax.rem(ctx, 2)
    core = lax.rem(dp, 2)
    chip = dp // 2
    inv_scale = 1.0 / math.sqrt(HEAD)

    def zed(step):
        return lax.rem(z + step + NZ, NZ)

    up = (dp, zed(1) * 2 + yl)
    down = (dp, zed(-1) * 2 + yl)
    pair = (dp, z * 2 + (1 - yl))
    far_dp = chip * 2 + (1 - core)
    twin = (far_dp, ctx)

    def ctx_peer(step):
        return lax.rem(ctx + step, 16)

    def chip_peer(step):
        return lax.rem(chip // 4 + step // 4, 4) * 4 + lax.rem(chip + step % 4, 4)

    started = []

    def send(src, dst, ss, rs, device):
        copy = Sent(
            pltpu.make_async_remote_copy(
                src_ref=src, dst_ref=dst, send_sem=ss, recv_sem=rs,
                device_id=device, device_id_type=MESH,
            )
        )
        started.append(copy)
        return copy

    def finish():
        for copy in started:
            copy.wait_recv()
            copy.wait_send()

    barrier = pltpu.get_barrier_semaphore()
    for step in range(1, 16):
        for device in (
            (dp, ctx_peer(step)),
            (far_dp, ctx_peer(step)),
            (chip_peer(step) * 2 + core, ctx),
        ):
            pl.semaphore_signal(barrier, inc=1, device_id=device, device_id_type=MESH)
    pl.semaphore_signal(barrier, inc=1, device_id=twin, device_id_type=MESH)

    mine = aligned(ctx, TOK)
    loads = [pltpu.make_async_copy(span_ref, spans, own_sem.at[8])]
    for n, (ref, start, width) in enumerate(
        [(k_ref, 0, 128), (v_ref, 128, 128), (q_ref, 256, 256), (do_ref, 512, 256)]
    ):
        for s in range(2):
            loads.append(
                pltpu.make_async_copy(
                    ref.at[0, pl.ds(s * SPAN, SPAN)],
                    raw.at[2 * ctx + s, :, pl.ds(start, width)],
                    own_sem.at[2 * n + s],
                )
            )
    for load in loads:
        load.start()
    for load in loads:
        load.wait()
    pl.semaphore_wait(barrier, 46)

    def ring_send(lane, step, view_up, view_down):
        return (
            send(view_up, view_up, ring_ss.at[lane, 0, step], ring_rs.at[lane, 0, step], up),
            send(view_down, view_down, ring_ss.at[lane, 1, step], ring_rs.at[lane, 1, step], down),
        )

    def forward(lane, place, block_z, columns):
        view = raw.at[pl.ds(block_z * 4 + yl * 2, 2), :, columns]
        return send(view, view, fwd_ss.at[lane, place], fwd_rs.at[lane, place], pair)

    forwards = []

    def z_first(lane, start, width):
        columns = pl.ds(start, width)
        half = width // 2

        def views(step):
            if step < 4:
                return (
                    raw.at[pl.ds(zed(1 - step) * 4 + yl * 2, 2), :, columns],
                    raw.at[pl.ds(zed(step - 1) * 4 + yl * 2, 2), :, columns],
                )
            return (
                raw.at[pl.ds(zed(-3) * 4 + yl * 2, 2), :, pl.ds(start, half)],
                raw.at[pl.ds(zed(3) * 4 + yl * 2, 2), :, pl.ds(start + half, half)],
            )

        copies = ring_send(lane, 1, *views(1))
        forwards.append(forward(lane, 0, z, columns))
        yield
        for step in range(1, 5):
            for copy in copies:
                copy.wait_recv()
            if step < 4:
                copies = ring_send(lane, step + 1, *views(step + 1))
                forwards.append(forward(lane, 2 * step - 1, zed(-step), columns))
                forwards.append(forward(lane, 2 * step, zed(step), columns))
            else:
                forwards.append(forward(lane, 7, zed(4), columns))
            yield

    def y_first(lane, start, width):
        columns = pl.ds(start, width)
        exchange = forward(lane, 0, z, columns)
        yield

        def views(step):
            if step < 4:
                return (
                    raw.at[pl.ds(zed(1 - step) * 4, 4), :, columns],
                    raw.at[pl.ds(zed(step - 1) * 4, 4), :, columns],
                )
            return (
                raw.at[pl.ds(zed(-3) * 4, 2), :, columns],
                raw.at[pl.ds(zed(3) * 4 + 2, 2), :, columns],
            )

        exchange.wait_recv()
        copies = ring_send(lane, 1, *views(1))
        yield
        for step in range(1, 5):
            for copy in copies:
                copy.wait_recv()
            if step < 4:
                copies = ring_send(lane, step + 1, *views(step + 1))
            yield

    lanes = [y_first(0, 0, 256), z_first(1, 256, 256), z_first(2, 512, 256)]
    for lane in lanes:
        next(lane)
    next(lanes[0])

    own_copy = pltpu.make_async_copy(
        h_ref.at[0, :, aligned(ctx, FEAT)], hid.at[mine, :], own_sem.at[9]
    )
    own_copy.start()

    def find_slot(block, carry):
        slot = jnp.int32(0)
        for s in range(32):
            slot = jnp.where(spans[0, s] == block, jnp.int32(s), slot)
        slots[block] = slot
        return carry

    lax.fori_loop(0, 32, find_slot, 0)
    for step in range(1, 5):
        for lane in lanes:
            next(lane)
    for copy in forwards:
        copy.wait_recv()

    hid_copies = []
    for ahead in [8, 9, 7, 10, 6, 11, 5, 12, 4, 13, 3, 14, 2, 15, 1]:
        peer = ctx_peer(ahead)
        hid_copies.append(
            send(
                h_ref.at[0, :, aligned(peer, FEAT)], hid.at[mine, :],
                hid_ss.at[ahead], hid_rs.at[ahead], (dp, peer),
            )
        )

    def place_block(block, carry):
        rows = raw[slots[block]]
        keys[aligned(block, SPAN), :] = rows[:, :128]
        values[aligned(block, SPAN), :] = rows[:, 128:256]
        tile = block // 4
        for h in range(2):
            into = aligned(h * 4 + lax.rem(block, 4), SPAN)
            queries[tile, into, :] = rows[:, 256 + h * 128 : 384 + h * 128]
            douts[tile, into, :] = rows[:, 512 + h * 128 : 640 + h * 128]
        return carry

    lax.fori_loop(0, 32, place_block, 0)
    keys_t[...] = keys[...].T
    key_acc[...] = jnp.zeros_like(key_acc)
    value_acc[...] = jnp.zeros_like(value_acc)

    to_log2 = inv_scale * math.log2(math.e)

    def query_tile(tile, carry):
        query = queries[tile]
        dout = douts[tile]

        def totals(block, running, diagonal=False):
            top, total, dot = running
            rows = aligned(block, 256)
            scores = contract(keys[rows, :], query, 1, 1) * to_log2
            if diagonal:
                key_at = lax.broadcasted_iota(jnp.int32, (256, 512), 0)
                query_at = lax.rem(lax.broadcasted_iota(jnp.int32, (256, 512), 1), 256)
                scores = jnp.where(key_at <= query_at, scores, masked_fill)
            probs = contract(values[rows, :], dout, 1, 1)
            here = jnp.max(scores, axis=0, keepdims=True)
            weights = jnp.exp2(scores - here)
            expo[rows, :] = weights
            dprob[rows, :] = probs
            tops[block] = jnp.broadcast_to(here, (8, 512))
            new_top = jnp.maximum(top, here)
            old, new = jnp.exp2(top - new_top), jnp.exp2(here - new_top)
            total = old * total + new * jnp.sum(weights, axis=0, keepdims=True)
            dot = old * dot + new * jnp.sum(weights * probs, axis=0, keepdims=True)
            return new_top, total, dot

        running = (
            jnp.full((1, 512), masked_fill, F32),
            jnp.zeros((1, 512), F32),
            jnp.zeros((1, 512), F32),
        )
        running = totals(tile, running, True)
        top, total, dot = lax.fori_loop(0, tile, totals, running)
        log_total = top + jnp.log2(total)
        row_delta = dot / total

        def gradients(block, query_sum):
            rows = aligned(block, 256)
            probs = expo[rows, :] * jnp.exp2(tops[block][0:1] - log_total)
            scores_low = (probs * (dprob[rows, :] - row_delta)).astype(BF16)
            value_acc[rows, :] += jnp.dot(
                probs.astype(BF16), dout, preferred_element_type=F32
            )
            key_acc[rows, :] += jnp.dot(scores_low, query, preferred_element_type=F32)
            return query_sum + jnp.dot(keys_t[:, rows], scores_low, preferred_element_type=F32)

        query_sum = lax.fori_loop(0, tile + 1, gradients, jnp.zeros((128, 512), F32))
        query_sum = (query_sum.T * inv_scale).astype(BF16)
        rows = pl.ds(tile * 4, 4)
        grads[rows, :, :128] = query_sum[:256].reshape(4, SPAN, 128)
        grads[rows, :, 128:256] = query_sum[256:].reshape(4, SPAN, 128)
        return carry

    lax.fori_loop(0, 8, query_tile, 0)
    grads[:, :, 256:384] = (key_acc[...] * inv_scale).astype(BF16).reshape(32, SPAN, 128)
    grads[:, :, 384:] = value_acc[...].astype(BF16).reshape(32, SPAN, 128)

    own_copy.wait()
    for copy in hid_copies:
        copy.wait_recv()

    for block in range(NZ):
        part = jnp.concatenate(
            [grads[spans[0, block * 4 + s]] for s in range(4)], axis=0
        )
        part = contract(hid[block * 256 : (block + 1) * 256, :], part, 0, 0)
        if block == 0:
            acc[...] = part
        else:
            acc[...] += part

    near_rows = aligned(core, TOK)
    half_copy = send(
        acc.at[aligned(1 - core, TOK)], half_in, twin_ss.at[0], twin_rs.at[0], twin
    )
    whole = acc[...]
    squares = jnp.sum((whole * whole).reshape(32, 8, COLS), axis=0)
    norm_box[ctx] = (
        squares[:, :128] + squares[:, 128:256] + squares[:, 256:384] + squares[:, 384:]
    )
    norm_copies = []
    for ahead in range(16):
        place = norm_box.at[ctx]
        if ahead:
            norm_copies.append(
                send(
                    place, place, norm_ss.at[0, ahead], norm_rs.at[0, ahead],
                    (dp, ctx_peer(ahead)),
                )
            )
        norm_copies.append(
            send(
                place, norm_far.at[ctx], norm_ss.at[1, ahead], norm_rs.at[1, ahead],
                (far_dp, ctx_peer(ahead)),
            )
        )
    for copy in norm_copies:
        copy.wait_recv()

    def factor_of(box):
        total_sq = jnp.sum(jnp.sum(box[...], axis=0), axis=(0, 1), keepdims=True)
        return scale_total / (jnp.sqrt(total_sq) + gamma_floor)

    near_factor = factor_of(norm_box)
    far_factor = factor_of(norm_far)
    half_copy.wait_recv()
    mixed = acc[near_rows, :] * near_factor + half_in[...] * far_factor
    for place in range(CHIPS):
        r, w = (place % 8) * 16, (place // 8) * FEAT
        rs_out[place] = mixed[r : r + 16, w : w + FEAT].astype(BF16)

    chip_order = [10, 8, 2, 9, 11, 6, 14, 5, 7, 13, 15, 4, 12, 1, 3]
    rs_copies = []
    for step in chip_order:
        other = chip_peer(step)
        rs_copies.append(
            send(
                rs_out.at[other], rs_in.at[chip], rs_ss.at[step], rs_rs.at[step],
                (other * 2 + core, ctx),
            )
        )
    rs_in[chip] = rs_out[chip]
    for copy in rs_copies:
        copy.wait_recv()

    piece = rs_in[0].astype(F32)
    for place in range(1, CHIPS):
        piece = piece + rs_in[place].astype(F32)
    ag[chip] = piece.astype(BF16)
    ag_copies = []
    for step in chip_order:
        other = chip_peer(step)
        ag_copies.append(
            send(
                ag.at[chip], ag.at[chip], ag_ss.at[step], ag_rs.at[step],
                (other * 2 + core, ctx),
            )
        )
    for copy in ag_copies:
        copy.wait_recv()

    last = send(ag, ag_far, twin_ss.at[1], twin_rs.at[1], twin)
    for place in range(CHIPS):
        r, w = (place % 8) * 16, (place // 8) * FEAT
        rows = pl.ds(pl.multiple_of(core * TOK + r, 16), 16)
        out_ref[rows, pl.ds(w, FEAT)] = ag[place].astype(F32)
    last.wait_recv()
    for place in range(CHIPS):
        r, w = (place % 8) * 16, (place // 8) * FEAT
        rows = pl.ds(pl.multiple_of((1 - core) * TOK + r, 16), 16)
        out_ref[rows, pl.ds(w, FEAT)] = ag_far[place].astype(F32)
    finish()


def on_device(hidden_in, query_states, key_states, value_states, out_grad, span_order):
    scale_total = math.sqrt(hidden_in.shape[2] * COLS / lax.axis_size("dp"))
    vmem = pl.BlockSpec(memory_space=pltpu.VMEM)
    dma = pltpu.SemaphoreType.DMA
    return pl.pallas_call(
        functools.partial(kernel, scale_total),
        name="clipped_grads",
        out_shape=jax.ShapeDtypeStruct((FEAT, COLS), F32),
        in_specs=[pl.BlockSpec(memory_space=pl.ANY)] * 6,
        out_specs=vmem,
        scratch_shapes=[
            pltpu.VMEM((16 * TOK, FEAT), BF16),
            pltpu.VMEM((32, SPAN, 6 * HEAD), BF16),
            pltpu.VMEM((16 * TOK, HEAD), BF16),
            pltpu.VMEM((HEAD, 16 * TOK), BF16),
            pltpu.VMEM((16 * TOK, HEAD), BF16),
            pltpu.VMEM((8, 512, HEAD), BF16),
            pltpu.VMEM((8, 512, HEAD), BF16),
            pltpu.VMEM((16 * TOK, 512), F32),
            pltpu.VMEM((16 * TOK, 512), F32),
            pltpu.VMEM((8, 8, 512), F32),
            pltpu.VMEM((16 * TOK, HEAD), F32),
            pltpu.VMEM((16 * TOK, HEAD), F32),
            pltpu.VMEM((32, SPAN, COLS), BF16),
            pltpu.VMEM((FEAT, COLS), F32),
            pltpu.VMEM((16, 8, 128), F32),
            pltpu.VMEM((16, 8, 128), F32),
            pltpu.VMEM((TOK, COLS), F32),
            pltpu.VMEM((CHIPS, 16, FEAT), BF16),
            pltpu.VMEM((CHIPS, 16, FEAT), BF16),
            pltpu.VMEM((CHIPS, 16, FEAT), BF16),
            pltpu.VMEM((CHIPS, 16, FEAT), BF16),
            pltpu.SMEM((1, 32), jnp.int32),
            pltpu.SMEM((32,), jnp.int32),
            dma((16,)), dma((16,)),
            dma((3, 2, 5)), dma((3, 2, 5)),
            dma((2,)), dma((2,)),
            dma((3, 8)), dma((3, 8)),
            dma((2, 16)), dma((2, 16)),
            dma((16,)), dma((16,)),
            dma((16,)), dma((16,)),
            dma((10,)),
        ],
        compiler_params=pltpu.CompilerParams(
            collective_id=0, has_side_effects=True, vmem_limit_bytes=62 << 20
        ),
    )(hidden_in, query_states, key_states, value_states, out_grad, span_order)


def solution(mesh):
    return jax.shard_map(
        on_device,
        mesh=mesh,
        in_specs=(
            P("dp", "ctx", None),
            P("dp", "ctx", None),
            P("dp", "ctx", None),
            P("dp", "ctx", None),
            P("dp", "ctx", None),
            P("dp", None),
        ),
        out_specs=P("ctx", None),
        check_vma=False,
    )
```

```python
import functools
import math

import jax
import jax.numpy as jnp
from jax import lax
from jax.experimental import pallas as pl
from jax.experimental.pallas import tpu as pltpu
from jax.sharding import PartitionSpec as P

MESH = pl.DeviceIdType.MESH
F32 = jnp.float32
BF16 = jnp.bfloat16

masked_fill = -1e30
gamma_floor = 0.01

TOK = 128
HEAD = 128
SPAN = 64
NZ = 8
FEAT = 256
COLS = 512
CHIPS = 16


def aligned(index, size):
    return pl.ds(pl.multiple_of(index * size, size), size)


def contract(left, right, left_dim, right_dim):
    return lax.dot_general(
        left, right, (((left_dim,), (right_dim,)), ((), ())), preferred_element_type=F32
    )


class Sent:
    def __init__(self, copy):
        self.copy = copy
        self.open_send = self.open_recv = True
        copy.start()

    def wait_recv(self):
        if self.open_recv:
            self.copy.wait_recv()
        self.open_recv = False

    def wait_send(self):
        if self.open_send:
            self.copy.wait_send()
        self.open_send = False


def kernel(
    scale_total,
    h_ref,
    q_ref,
    k_ref,
    v_ref,
    do_ref,
    span_ref,
    out_ref,
    hid,
    raw,
    keys,
    keys_t,
    values,
    queries,
    douts,
    expo,
    dprob,
    tops,
    key_acc,
    value_acc,
    query_acc,
    grads,
    acc,
    norm_box,
    fac,
    rs_out,
    rs_in,
    ag,
    ag_far,
    spans,
    slots,
    hid_ss,
    hid_rs,
    ring_ss,
    ring_rs,
    twin_ss,
    twin_rs,
    fwd_ss,
    fwd_rs,
    norm_ss,
    norm_rs,
    fac_ss,
    fac_rs,
    rs_ss,
    rs_rs,
    ag_ss,
    ag_rs,
    own_sem,
):
    dp = lax.axis_index("dp")
    ctx = lax.axis_index("ctx")
    z = ctx // 2
    yl = lax.rem(ctx, 2)
    core = lax.rem(dp, 2)
    chip = dp // 2
    inv_scale = 1.0 / math.sqrt(HEAD)

    def zed(step):
        return lax.rem(z + step + NZ, NZ)

    up = (dp, zed(1) * 2 + yl)
    down = (dp, zed(-1) * 2 + yl)
    pair = (dp, z * 2 + (1 - yl))
    twin = (chip * 2 + (1 - core), ctx)

    def ctx_peer(step):
        return lax.rem(ctx + step, 16)

    def chip_peer(step):
        return lax.rem(chip // 4 + step // 4, 4) * 4 + lax.rem(chip + step % 4, 4)

    ctx_order = [8, 9, 7, 10, 6, 11, 5, 12, 4, 13, 3, 14, 2, 15, 1]
    started = []

    def send(src, dst, ss, rs, device):
        copy = Sent(
            pltpu.make_async_remote_copy(
                src_ref=src, dst_ref=dst, send_sem=ss, recv_sem=rs,
                device_id=device, device_id_type=MESH,
            )
        )
        started.append(copy)
        return copy

    def finish():
        for copy in started:
            copy.wait_recv()
            copy.wait_send()

    barrier = pltpu.get_barrier_semaphore()
    for step in range(1, 16):
        for device in (
            (dp, ctx_peer(step)),
            (chip_peer(step) * 2, ctx),
            (chip_peer(step) * 2 + 1, ctx),
        ):
            pl.semaphore_signal(barrier, inc=1, device_id=device, device_id_type=MESH)
    pl.semaphore_signal(barrier, inc=1, device_id=twin, device_id_type=MESH)

    mine = aligned(ctx, TOK)
    loads = [pltpu.make_async_copy(span_ref, spans, own_sem.at[8])]
    for n, (ref, start, width) in enumerate(
        [(k_ref, 0, 128), (v_ref, 128, 128), (q_ref, 256, 256), (do_ref, 512, 256)]
    ):
        for s in range(2):
            loads.append(
                pltpu.make_async_copy(
                    ref.at[0, pl.ds(s * SPAN, SPAN)],
                    raw.at[2 * ctx + s, :, pl.ds(start, width)],
                    own_sem.at[2 * n + s],
                )
            )
    for load in loads:
        load.start()
    for load in loads:
        load.wait()
    pl.semaphore_wait(barrier, 46)

    def ring_send(lane, step, view_up, view_down):
        return (
            send(view_up, view_up, ring_ss.at[lane, 0, step], ring_rs.at[lane, 0, step], up),
            send(view_down, view_down, ring_ss.at[lane, 1, step], ring_rs.at[lane, 1, step], down),
        )

    def forward(lane, place, block_z, columns):
        view = raw.at[pl.ds(block_z * 4 + yl * 2, 2), :, columns]
        return send(view, view, fwd_ss.at[lane, place], fwd_rs.at[lane, place], pair)

    forwards = []

    def z_first(lane, start, width):
        columns = pl.ds(start, width)

        def views(step):
            if step < 4:
                return (
                    raw.at[pl.ds(zed(1 - step) * 4 + yl * 2, 2), :, columns],
                    raw.at[pl.ds(zed(step - 1) * 4 + yl * 2, 2), :, columns],
                )
            return (
                raw.at[zed(-3) * 4 + yl * 2, :, columns],
                raw.at[zed(3) * 4 + yl * 2 + 1, :, columns],
            )

        copies = ring_send(lane, 1, *views(1))
        forwards.append(forward(lane, 0, z, columns))
        yield
        for step in range(1, 5):
            for copy in copies:
                copy.wait_recv()
            if step < 4:
                copies = ring_send(lane, step + 1, *views(step + 1))
                forwards.append(forward(lane, 2 * step - 1, zed(-step), columns))
                forwards.append(forward(lane, 2 * step, zed(step), columns))
            else:
                forwards.append(forward(lane, 7, zed(4), columns))
            yield

    def y_first(lane, start, width):
        columns = pl.ds(start, width)
        exchange = forward(lane, 0, z, columns)
        yield

        def views(step):
            if step < 4:
                return (
                    raw.at[pl.ds(zed(1 - step) * 4, 4), :, columns],
                    raw.at[pl.ds(zed(step - 1) * 4, 4), :, columns],
                )
            return (
                raw.at[pl.ds(zed(-3) * 4, 2), :, columns],
                raw.at[pl.ds(zed(3) * 4 + 2, 2), :, columns],
            )

        exchange.wait_recv()
        copies = ring_send(lane, 1, *views(1))
        yield
        for step in range(1, 5):
            for copy in copies:
                copy.wait_recv()
            if step < 4:
                copies = ring_send(lane, step + 1, *views(step + 1))
            yield

    lanes = [y_first(0, 0, 256), z_first(1, 256, 256), z_first(2, 512, 256)]
    for lane in lanes:
        next(lane)
    for lane in lanes[:1]:
        next(lane)

    own_copy = pltpu.make_async_copy(
        h_ref.at[0, :, aligned(ctx, FEAT)], hid.at[mine, :], own_sem.at[9]
    )
    own_copy.start()

    def find_slot(block, carry):
        slot = jnp.int32(0)
        for s in range(32):
            slot = jnp.where(spans[0, s] == block, jnp.int32(s), slot)
        slots[block] = slot
        return carry

    lax.fori_loop(0, 32, find_slot, 0)
    hid_copies = []

    def send_features(aheads):
        for ahead in aheads:
            peer = ctx_peer(ahead)
            hid_copies.append(
                send(
                    h_ref.at[0, :, aligned(peer, FEAT)], hid.at[mine, :],
                    hid_ss.at[ahead], hid_rs.at[ahead], (dp, peer),
                )
            )

    early = {1: [2, 14], 2: [3, 15], 3: [1]}
    for step in range(1, 5):
        for lane in lanes:
            next(lane)
        send_features(early.get(step, []))
    for copy in forwards:
        copy.wait_recv()

    send_features([8, 9, 7, 10, 6, 11, 5, 12, 4, 13])

    def place_block(block, carry):
        rows = raw[slots[block]]
        keys[aligned(block, SPAN), :] = rows[:, :128]
        values[aligned(block, SPAN), :] = rows[:, 128:256]
        tile = block // 4
        for h in range(2):
            into = aligned(h * 4 + lax.rem(block, 4), SPAN)
            queries[tile, into, :] = rows[:, 256 + h * 128 : 384 + h * 128]
            douts[tile, into, :] = rows[:, 512 + h * 128 : 640 + h * 128]
        return carry

    lax.fori_loop(0, 32, place_block, 0)
    keys_t[...] = keys[...].T

    to_log2 = inv_scale * math.log2(math.e)

    def totals(tile, block, head, running):
        top, total, dot = running
        lanes = pl.ds(head * 256, 256)
        query, dout = queries[tile, lanes, :], douts[tile, lanes, :]
        for part in range(2):
            rows = pl.ds(block * 256 + part * 128, 128)
            scores = contract(keys[rows, :], query, 1, 1) * to_log2
            if block == tile:
                key_at = lax.broadcasted_iota(jnp.int32, (128, 256), 0) + part * 128
                query_at = lax.broadcasted_iota(jnp.int32, (128, 256), 1)
                scores = jnp.where(key_at <= query_at, scores, masked_fill)
            probs = contract(values[rows, :], dout, 1, 1)
            here = jnp.max(scores, axis=0, keepdims=True)
            weights = jnp.exp2(scores - here)
            expo[rows, lanes] = weights
            dprob[rows, lanes] = probs
            tops[block * 2 + part, :, lanes] = jnp.broadcast_to(here, (8, 256))
            new_top = jnp.maximum(top, here)
            old, new = jnp.exp2(top - new_top), jnp.exp2(here - new_top)
            total = old * total + new * jnp.sum(weights, axis=0, keepdims=True)
            dot = old * dot + new * jnp.sum(weights * probs, axis=0, keepdims=True)
            top = new_top
        return top, total, dot

    def gradients(tile, block, log_total, row_delta):
        probs = jnp.concatenate(
            [
                expo[pl.ds(block * 256 + part * 128, 128), :]
                * jnp.exp2(tops[block * 2 + part, 0:1, :] - log_total)
                for part in range(2)
            ],
            axis=0,
        )
        rows = pl.ds(block * 256, 256)
        scores_low = (probs * (dprob[rows, :] - row_delta)).astype(BF16)
        value_add = jnp.dot(probs.astype(BF16), douts[tile], preferred_element_type=F32)
        key_add = jnp.dot(scores_low, queries[tile], preferred_element_type=F32)
        if tile == block:
            value_acc[rows, :] = value_add
            key_acc[rows, :] = key_add
        else:
            value_acc[rows, :] += value_add
            key_acc[rows, :] += key_add
        return jnp.dot(keys_t[:, rows], scores_low, preferred_element_type=F32)

    for tile in range(8):
        heads = []
        for head in range(2):
            running = (
                jnp.full((1, 256), masked_fill, F32),
                jnp.zeros((1, 256), F32),
                jnp.zeros((1, 256), F32),
            )
            for block in [tile, *range(tile)]:
                running = totals(tile, block, head, running)
            heads.append(running)
        top, total, dot = (jnp.concatenate(both, axis=1) for both in zip(*heads))
        log_total = top + jnp.log2(total)
        row_delta = dot / total
        for block in range(tile + 1):
            query_add = gradients(tile, block, log_total, row_delta)
            if block == 0:
                query_acc[...] = query_add
            else:
                query_acc[...] += query_add
        query_sum = (query_acc[...].T * inv_scale).astype(BF16)
        rows = pl.ds(tile * 4, 4)
        grads[rows, :, :128] = query_sum[:256].reshape(4, SPAN, 128)
        grads[rows, :, 128:256] = query_sum[256:].reshape(4, SPAN, 128)

    grads[:, :, 256:384] = (key_acc[...] * inv_scale).astype(BF16).reshape(32, SPAN, 128)
    grads[:, :, 384:] = value_acc[...].astype(BF16).reshape(32, SPAN, 128)

    own_copy.wait()
    for copy in hid_copies:
        copy.wait_recv()

    for block in range(NZ):
        part = jnp.concatenate(
            [grads[spans[0, block * 4 + s]] for s in range(4)], axis=0
        )
        part = contract(hid[block * 256 : (block + 1) * 256, :], part, 0, 0)
        if block == 0:
            acc[...] = part
        else:
            acc[...] += part

    whole = acc[...]
    squares = jnp.sum((whole * whole).reshape(32, 8, COLS), axis=0)
    norm_box[ctx] = (
        squares[:, :128] + squares[:, 128:256] + squares[:, 256:384] + squares[:, 384:]
    )
    norm_copies = []
    for ahead in ctx_order:
        place = norm_box.at[ctx]
        norm_copies.append(
            send(place, place, norm_ss.at[ahead], norm_rs.at[ahead], (dp, ctx_peer(ahead)))
        )

    for place in range(32):
        r, w = (place // 2) * 16, (place % 2) * FEAT
        rs_out[place] = whole[r : r + 16, w : w + FEAT].astype(BF16)
    chip_order = [10, 8, 2, 9, 11, 6, 14, 5, 7, 13, 15, 4, 12, 1, 3, 0]
    rs_copies = []
    for step in chip_order:
        for side in range(2):
            if step == 0 and side == 0:
                continue
            other = chip_peer(step) * 2 + lax.rem(core + side, 2)
            rs_copies.append(
                send(
                    rs_out.at[other], rs_in.at[dp], rs_ss.at[step * 2 + side],
                    rs_rs.at[step * 2 + side], (other, ctx),
                )
            )
    rs_in[dp] = rs_out[dp]
    for copy in norm_copies:
        copy.wait_recv()

    total_sq = jnp.sum(jnp.sum(norm_box[...], axis=0), axis=(0, 1), keepdims=True)
    factor = scale_total / (jnp.sqrt(total_sq) + gamma_floor)
    fac[dp] = jnp.broadcast_to(factor, (8, 128))
    fac_copies = []
    for step in chip_order:
        for side in range(2):
            if step == 0 and side == 0:
                continue
            other = chip_peer(step) * 2 + lax.rem(core + side, 2)
            fac_copies.append(
                send(
                    fac.at[dp], fac.at[dp], fac_ss.at[step * 2 + side],
                    fac_rs.at[step * 2 + side], (other, ctx),
                )
            )

    for copy in rs_copies + fac_copies:
        copy.wait_recv()

    piece = jnp.zeros((16, FEAT), F32)
    for place in range(32):
        row = fac[place, 0:1, :]
        piece += rs_in[place].astype(F32) * jnp.concatenate([row, row], axis=1)
    ag[chip] = piece.astype(BF16)
    ag_copies = []
    for step in chip_order[:-1]:
        other = chip_peer(step)
        ag_copies.append(
            send(
                ag.at[chip], ag.at[chip], ag_ss.at[step], ag_rs.at[step],
                (other * 2 + core, ctx),
            )
        )
    for copy in ag_copies:
        copy.wait_recv()

    last = send(ag, ag_far, twin_ss.at[0], twin_rs.at[0], twin)
    for place in range(CHIPS):
        out_ref[place * 16 : place * 16 + 16, aligned(core, FEAT)] = ag[place].astype(F32)
    last.wait_recv()
    for place in range(CHIPS):
        out_ref[place * 16 : place * 16 + 16, aligned(1 - core, FEAT)] = ag_far[place].astype(F32)
    finish()


def on_device(hidden_in, query_states, key_states, value_states, out_grad, span_order):
    scale_total = math.sqrt(hidden_in.shape[2] * COLS / lax.axis_size("dp"))
    vmem = pl.BlockSpec(memory_space=pltpu.VMEM)
    dma = pltpu.SemaphoreType.DMA
    return pl.pallas_call(
        functools.partial(kernel, scale_total),
        name="clipped_grads",
        out_shape=jax.ShapeDtypeStruct((FEAT, COLS), F32),
        in_specs=[pl.BlockSpec(memory_space=pl.ANY)] * 6,
        out_specs=vmem,
        scratch_shapes=[
            pltpu.VMEM((16 * TOK, FEAT), BF16),
            pltpu.VMEM((32, SPAN, 6 * HEAD), BF16),
            pltpu.VMEM((16 * TOK, HEAD), BF16),
            pltpu.VMEM((HEAD, 16 * TOK), BF16),
            pltpu.VMEM((16 * TOK, HEAD), BF16),
            pltpu.VMEM((8, 512, HEAD), BF16),
            pltpu.VMEM((8, 512, HEAD), BF16),
            pltpu.VMEM((16 * TOK, 512), F32),
            pltpu.VMEM((16 * TOK, 512), F32),
            pltpu.VMEM((16, 8, 512), F32),
            pltpu.VMEM((16 * TOK, HEAD), F32),
            pltpu.VMEM((16 * TOK, HEAD), F32),
            pltpu.VMEM((HEAD, 512), F32),
            pltpu.VMEM((32, SPAN, COLS), BF16),
            pltpu.VMEM((FEAT, COLS), F32),
            pltpu.VMEM((16, 8, 128), F32),
            pltpu.VMEM((32, 8, 128), F32),
            pltpu.VMEM((32, 16, FEAT), BF16),
            pltpu.VMEM((32, 16, FEAT), BF16),
            pltpu.VMEM((CHIPS, 16, FEAT), BF16),
            pltpu.VMEM((CHIPS, 16, FEAT), BF16),
            pltpu.SMEM((1, 32), jnp.int32),
            pltpu.SMEM((32,), jnp.int32),
            dma((16,)), dma((16,)),
            dma((6, 2, 5)), dma((6, 2, 5)),
            dma((2,)), dma((2,)),
            dma((6, 8)), dma((6, 8)),
            dma((16,)), dma((16,)),
            dma((32,)), dma((32,)),
            dma((32,)), dma((32,)),
            dma((16,)), dma((16,)),
            dma((10,)),
        ],
        compiler_params=pltpu.CompilerParams(
            collective_id=0, has_side_effects=True, vmem_limit_bytes=62 << 20
        ),
    )(hidden_in, query_states, key_states, value_states, out_grad, span_order)


def solution(mesh):
    return jax.shard_map(
        on_device,
        mesh=mesh,
        in_specs=(
            P("dp", "ctx", None),
            P("dp", "ctx", None),
            P("dp", "ctx", None),
            P("dp", "ctx", None),
            P("dp", "ctx", None),
            P("dp", None),
        ),
        out_specs=P("ctx", None),
        check_vma=False,
    )
```

```python
import functools
import math

import jax
import jax.numpy as jnp
from jax import lax
from jax.experimental import pallas as pl
from jax.experimental.pallas import tpu as pltpu
from jax.sharding import PartitionSpec as P

MESH = pl.DeviceIdType.MESH
F32 = jnp.float32
BF16 = jnp.bfloat16

masked_fill = -1e30
gamma_floor = 0.01

TOK = 128
HEAD = 128
SPAN = 64
NZ = 8
FEAT = 256
COLS = 512
CHIPS = 16


def aligned(index, size):
    return pl.ds(pl.multiple_of(index * size, size), size)


def contract(left, right, left_dim, right_dim):
    return lax.dot_general(
        left, right, (((left_dim,), (right_dim,)), ((), ())), preferred_element_type=F32
    )


class Sent:
    def __init__(self, copy):
        self.copy = copy
        self.open_send = self.open_recv = True
        copy.start()

    def wait_recv(self):
        if self.open_recv:
            self.copy.wait_recv()
        self.open_recv = False

    def wait_send(self):
        if self.open_send:
            self.copy.wait_send()
        self.open_send = False


def kernel(
    scale_total,
    h_ref,
    q_ref,
    k_ref,
    v_ref,
    do_ref,
    span_ref,
    out_ref,
    hid,
    raw,
    keys,
    keys_t,
    values,
    queries,
    douts,
    expo,
    dprob,
    tops,
    key_acc,
    value_acc,
    query_acc,
    grads,
    acc,
    norm_box,
    norm_far,
    half_in,
    rs_out,
    rs_in,
    ag,
    spans,
    slots,
    hid_ss,
    hid_rs,
    ring_ss,
    ring_rs,
    twin_ss,
    twin_rs,
    fwd_ss,
    fwd_rs,
    norm_ss,
    norm_rs,
    rs_ss,
    rs_rs,
    ag_ss,
    ag_rs,
    own_sem,
):
    dp = lax.axis_index("dp")
    ctx = lax.axis_index("ctx")
    z = ctx // 2
    yl = lax.rem(ctx, 2)
    core = lax.rem(dp, 2)
    chip = dp // 2
    inv_scale = 1.0 / math.sqrt(HEAD)

    def zed(step):
        return lax.rem(z + step + NZ, NZ)

    up = (dp, zed(1) * 2 + yl)
    down = (dp, zed(-1) * 2 + yl)
    pair = (dp, z * 2 + (1 - yl))
    far_dp = chip * 2 + (1 - core)
    twin = (far_dp, ctx)

    def ctx_peer(step):
        return lax.rem(ctx + step, 16)

    def chip_peer(step):
        return lax.rem(chip // 4 + step // 4, 4) * 4 + lax.rem(chip + step % 4, 4)

    ctx_order = [8, 9, 7, 10, 6, 11, 5, 12, 4, 13, 3, 14, 2, 15, 1]
    started = []

    def send(src, dst, ss, rs, device):
        copy = Sent(
            pltpu.make_async_remote_copy(
                src_ref=src, dst_ref=dst, send_sem=ss, recv_sem=rs,
                device_id=device, device_id_type=MESH,
            )
        )
        started.append(copy)
        return copy

    def finish():
        for copy in started:
            copy.wait_recv()
            copy.wait_send()

    mine = aligned(ctx, TOK)
    loads = [pltpu.make_async_copy(span_ref, spans, own_sem.at[8])]
    for n, (ref, start, width) in enumerate(
        [(k_ref, 0, 128), (v_ref, 128, 128), (q_ref, 256, 256), (do_ref, 512, 256)]
    ):
        for s in range(2):
            loads.append(
                pltpu.make_async_copy(
                    ref.at[0, pl.ds(s * SPAN, SPAN)],
                    raw.at[2 * ctx + s, :, pl.ds(start, width)],
                    own_sem.at[2 * n + s],
                )
            )
    for load in loads:
        load.start()

    barrier = pltpu.get_barrier_semaphore()
    for step in ctx_order:
        for device in (
            (dp, ctx_peer(step)),
            (far_dp, ctx_peer(step)),
            (chip_peer(step) * 2 + core, ctx),
        ):
            pl.semaphore_signal(barrier, inc=1, device_id=device, device_id_type=MESH)
    pl.semaphore_signal(barrier, inc=1, device_id=twin, device_id_type=MESH)
    for load in loads:
        load.wait()
    pl.semaphore_wait(barrier, 46)

    def ring_send(lane, step, view_up, view_down):
        return (
            send(view_up, view_up, ring_ss.at[lane, 0, step], ring_rs.at[lane, 0, step], up),
            send(view_down, view_down, ring_ss.at[lane, 1, step], ring_rs.at[lane, 1, step], down),
        )

    def forward(lane, place, block_z, columns):
        view = raw.at[pl.ds(block_z * 4 + yl * 2, 2), :, columns]
        return send(view, view, fwd_ss.at[lane, place], fwd_rs.at[lane, place], pair)

    forwards = []

    def z_first(lane, start, width):
        columns = pl.ds(start, width)

        def views(step):
            if step < 4:
                return (
                    raw.at[pl.ds(zed(1 - step) * 4 + yl * 2, 2), :, columns],
                    raw.at[pl.ds(zed(step - 1) * 4 + yl * 2, 2), :, columns],
                )
            return (
                raw.at[zed(-3) * 4 + yl * 2, :, columns],
                raw.at[zed(3) * 4 + yl * 2 + 1, :, columns],
            )

        copies = ring_send(lane, 1, *views(1))
        forwards.append(forward(lane, 0, z, columns))
        yield
        for step in range(1, 5):
            for copy in copies:
                copy.wait_recv()
            if step < 4:
                copies = ring_send(lane, step + 1, *views(step + 1))
                forwards.append(forward(lane, 2 * step - 1, zed(-step), columns))
                forwards.append(forward(lane, 2 * step, zed(step), columns))
            else:
                forwards.append(forward(lane, 7, zed(4), columns))
            yield

    def y_first(lane, start, width):
        columns = pl.ds(start, width)
        exchange = forward(lane, 0, z, columns)
        yield

        def views(step):
            if step < 4:
                return (
                    raw.at[pl.ds(zed(1 - step) * 4, 4), :, columns],
                    raw.at[pl.ds(zed(step - 1) * 4, 4), :, columns],
                )
            return (
                raw.at[pl.ds(zed(-3) * 4, 2), :, columns],
                raw.at[pl.ds(zed(3) * 4 + 2, 2), :, columns],
            )

        exchange.wait_recv()
        copies = ring_send(lane, 1, *views(1))
        yield
        for step in range(1, 5):
            for copy in copies:
                copy.wait_recv()
            if step < 4:
                copies = ring_send(lane, step + 1, *views(step + 1))
            yield

    lanes = [y_first(0, 0, 256), z_first(1, 256, 256), z_first(2, 512, 256)]
    for lane in lanes:
        next(lane)
    for lane in lanes[:1]:
        next(lane)

    own_copy = pltpu.make_async_copy(
        h_ref.at[0, :, aligned(ctx, FEAT)], hid.at[mine, :], own_sem.at[9]
    )
    own_copy.start()

    def find_slot(block, carry):
        slot = jnp.int32(0)
        for s in range(32):
            slot = jnp.where(spans[0, s] == block, jnp.int32(s), slot)
        slots[block] = slot
        return carry

    lax.fori_loop(0, 32, find_slot, 0)
    hid_copies = []

    def send_features(aheads):
        for ahead in aheads:
            peer = ctx_peer(ahead)
            hid_copies.append(
                send(
                    h_ref.at[0, :, aligned(peer, FEAT)], hid.at[mine, :],
                    hid_ss.at[ahead], hid_rs.at[ahead], (dp, peer),
                )
            )

    early = {3: [8], 4: [6, 10, 4, 12, 2, 14]}
    for step in range(1, 5):
        for lane in lanes:
            next(lane)
        send_features(early.get(step, []))
    for copy in forwards:
        copy.wait_recv()

    send_features([9, 7, 11, 5, 13, 3, 15, 1])

    def place_block(block, carry):
        rows = raw[slots[block]]
        keys[aligned(block, SPAN), :] = rows[:, :128]
        values[aligned(block, SPAN), :] = rows[:, 128:256]
        tile = block // 4
        for h in range(2):
            into = aligned(h * 4 + lax.rem(block, 4), SPAN)
            queries[tile, into, :] = rows[:, 256 + h * 128 : 384 + h * 128]
            douts[tile, into, :] = rows[:, 512 + h * 128 : 640 + h * 128]
        return carry

    lax.fori_loop(0, 32, place_block, 0)
    keys_t[...] = keys[...].T

    to_log2 = inv_scale * math.log2(math.e)

    def totals(tile, block, head, running):
        top, total, dot = running
        lanes = pl.ds(head * 256, 256)
        query, dout = queries[tile, lanes, :], douts[tile, lanes, :]
        for part in range(2):
            rows = pl.ds(block * 256 + part * 128, 128)
            scores = contract(keys[rows, :], query, 1, 1) * to_log2
            if block == tile:
                key_at = lax.broadcasted_iota(jnp.int32, (128, 256), 0) + part * 128
                query_at = lax.broadcasted_iota(jnp.int32, (128, 256), 1)
                scores = jnp.where(key_at <= query_at, scores, masked_fill)
            probs = contract(values[rows, :], dout, 1, 1)
            here = jnp.max(scores, axis=0, keepdims=True)
            weights = jnp.exp2(scores - here)
            expo[rows, lanes] = weights
            dprob[rows, lanes] = probs
            tops[block * 2 + part, :, lanes] = jnp.broadcast_to(here, (8, 256))
            new_top = jnp.maximum(top, here)
            old, new = jnp.exp2(top - new_top), jnp.exp2(here - new_top)
            total = old * total + new * jnp.sum(weights, axis=0, keepdims=True)
            dot = old * dot + new * jnp.sum(weights * probs, axis=0, keepdims=True)
            top = new_top
        return top, total, dot

    def gradients(tile, block, log_total, row_delta):
        probs = jnp.concatenate(
            [
                expo[pl.ds(block * 256 + part * 128, 128), :]
                * jnp.exp2(tops[block * 2 + part, 0:1, :] - log_total)
                for part in range(2)
            ],
            axis=0,
        )
        rows = pl.ds(block * 256, 256)
        scores_low = (probs * (dprob[rows, :] - row_delta)).astype(BF16)
        value_add = jnp.dot(probs.astype(BF16), douts[tile], preferred_element_type=F32)
        key_add = jnp.dot(scores_low, queries[tile], preferred_element_type=F32)
        if tile == block:
            value_acc[rows, :] = value_add
            key_acc[rows, :] = key_add
        else:
            value_acc[rows, :] += value_add
            key_acc[rows, :] += key_add
        return jnp.dot(keys_t[:, rows], scores_low, preferred_element_type=F32)

    for tile in range(8):
        heads = []
        for head in range(2):
            running = (
                jnp.full((1, 256), masked_fill, F32),
                jnp.zeros((1, 256), F32),
                jnp.zeros((1, 256), F32),
            )
            for block in [tile, *range(tile)]:
                running = totals(tile, block, head, running)
            heads.append(running)
        top, total, dot = (jnp.concatenate(both, axis=1) for both in zip(*heads))
        log_total = top + jnp.log2(total)
        row_delta = dot / total
        for block in range(tile + 1):
            query_add = gradients(tile, block, log_total, row_delta)
            if block == 0:
                query_acc[...] = query_add
            else:
                query_acc[...] += query_add
        query_sum = (query_acc[...].T * inv_scale).astype(BF16)
        rows = pl.ds(tile * 4, 4)
        grads[rows, :, :128] = query_sum[:256].reshape(4, SPAN, 128)
        grads[rows, :, 128:256] = query_sum[256:].reshape(4, SPAN, 128)

    grads[:, :, 256:384] = (key_acc[...] * inv_scale).astype(BF16).reshape(32, SPAN, 128)
    grads[:, :, 384:] = value_acc[...].astype(BF16).reshape(32, SPAN, 128)

    own_copy.wait()
    for copy in hid_copies:
        copy.wait_recv()

    for block in range(NZ):
        part = jnp.concatenate(
            [grads[spans[0, block * 4 + s]] for s in range(4)], axis=0
        )
        part = contract(hid[block * 256 : (block + 1) * 256, :], part, 0, 0)
        if block == 0:
            acc[...] = part
        else:
            acc[...] += part

    half_copy = send(
        acc.at[:, aligned(1 - core, FEAT)], half_in, twin_ss.at[0], twin_rs.at[0], twin
    )
    whole = acc[...]
    squares = jnp.sum((whole * whole).reshape(32, 8, COLS), axis=0)
    norm_box[ctx] = (
        squares[:, :128] + squares[:, 128:256] + squares[:, 256:384] + squares[:, 384:]
    )
    norm_copies = []
    for ahead in ctx_order + [0]:
        place = norm_box.at[ctx]
        if ahead:
            norm_copies.append(
                send(
                    place, place, norm_ss.at[0, ahead], norm_rs.at[0, ahead],
                    (dp, ctx_peer(ahead)),
                )
            )
        norm_copies.append(
            send(
                place, norm_far.at[ctx], norm_ss.at[1, ahead], norm_rs.at[1, ahead],
                (far_dp, ctx_peer(ahead)),
            )
        )
    for copy in norm_copies:
        copy.wait_recv()

    def factor_of(box):
        total_sq = jnp.sum(jnp.sum(box[...], axis=0), axis=(0, 1), keepdims=True)
        return scale_total / (jnp.sqrt(total_sq) + gamma_floor)

    near_factor = factor_of(norm_box)
    far_factor = factor_of(norm_far)
    half_copy.wait_recv()
    mixed = acc[:, aligned(core, FEAT)] * near_factor + half_in[...] * far_factor
    rs_out[...] = mixed.astype(BF16).reshape(CHIPS, 16, FEAT)

    chip_order = [10, 8, 2, 9, 11, 6, 14, 5, 7, 13, 15, 4, 12, 1, 3]
    rs_copies = []
    for step in chip_order:
        other = chip_peer(step)
        rs_copies.append(
            send(
                rs_out.at[other], rs_in.at[chip], rs_ss.at[step], rs_rs.at[step],
                (other * 2 + core, ctx),
            )
        )
    rs_in[chip] = rs_out[chip]
    for copy in rs_copies:
        copy.wait_recv()

    piece = rs_in[0].astype(F32)
    for place in range(1, CHIPS):
        piece += rs_in[place].astype(F32)
    ag[chip] = piece.astype(BF16)
    ag_copies = []
    for step in chip_order:
        other = chip_peer(step)
        ag_copies.append(
            send(
                ag.at[chip], ag.at[chip], ag_ss.at[step], ag_rs.at[step],
                (other * 2 + core, ctx),
            )
        )
    for copy in ag_copies:
        copy.wait_recv()

    half = out_ref.at[:, :, aligned(core, FEAT)]
    send(ag, half, twin_ss.at[1], twin_rs.at[1], twin)
    keep = pltpu.make_async_copy(ag, half, own_sem.at[10])
    keep.start()
    keep.wait()
    finish()


def on_device(hidden_in, query_states, key_states, value_states, out_grad, span_order):
    scale_total = math.sqrt(hidden_in.shape[2] * COLS / lax.axis_size("dp"))
    dma = pltpu.SemaphoreType.DMA
    summed = pl.pallas_call(
        functools.partial(kernel, scale_total),
        name="clipped_grads",
        out_shape=jax.ShapeDtypeStruct((CHIPS, 16, COLS), BF16),
        in_specs=[pl.BlockSpec(memory_space=pl.ANY)] * 6,
        out_specs=pl.BlockSpec(memory_space=pl.ANY),
        scratch_shapes=[
            pltpu.VMEM((16 * TOK, FEAT), BF16),
            pltpu.VMEM((32, SPAN, 6 * HEAD), BF16),
            pltpu.VMEM((16 * TOK, HEAD), BF16),
            pltpu.VMEM((HEAD, 16 * TOK), BF16),
            pltpu.VMEM((16 * TOK, HEAD), BF16),
            pltpu.VMEM((8, 512, HEAD), BF16),
            pltpu.VMEM((8, 512, HEAD), BF16),
            pltpu.VMEM((16 * TOK, 512), F32),
            pltpu.VMEM((16 * TOK, 512), F32),
            pltpu.VMEM((16, 8, 512), F32),
            pltpu.VMEM((16 * TOK, HEAD), F32),
            pltpu.VMEM((16 * TOK, HEAD), F32),
            pltpu.VMEM((HEAD, 512), F32),
            pltpu.VMEM((32, SPAN, COLS), BF16),
            pltpu.VMEM((FEAT, COLS), F32),
            pltpu.VMEM((16, 8, 128), F32),
            pltpu.VMEM((16, 8, 128), F32),
            pltpu.VMEM((FEAT, FEAT), F32),
            pltpu.VMEM((CHIPS, 16, FEAT), BF16),
            pltpu.VMEM((CHIPS, 16, FEAT), BF16),
            pltpu.VMEM((CHIPS, 16, FEAT), BF16),
            pltpu.SMEM((1, 32), jnp.int32),
            pltpu.SMEM((32,), jnp.int32),
            dma((16,)), dma((16,)),
            dma((6, 2, 5)), dma((6, 2, 5)),
            dma((2,)), dma((2,)),
            dma((6, 8)), dma((6, 8)),
            dma((2, 16)), dma((2, 16)),
            dma((16,)), dma((16,)),
            dma((16,)), dma((16,)),
            dma((11,)),
        ],
        compiler_params=pltpu.CompilerParams(
            collective_id=0, has_side_effects=True, vmem_limit_bytes=62 << 20
        ),
    )(hidden_in, query_states, key_states, value_states, out_grad, span_order)
    return summed.astype(F32).reshape(FEAT, COLS)


def solution(mesh):
    return jax.shard_map(
        on_device,
        mesh=mesh,
        in_specs=(
            P("dp", "ctx", None),
            P("dp", "ctx", None),
            P("dp", "ctx", None),
            P("dp", "ctx", None),
            P("dp", "ctx", None),
            P("dp", None),
        ),
        out_specs=P("ctx", None),
        check_vma=False,
    )
```

```python
import functools
import math

import jax
import jax.numpy as jnp
from jax import lax
from jax.experimental import pallas as pl
from jax.experimental.pallas import tpu as pltpu
from jax.sharding import PartitionSpec as P

MESH = pl.DeviceIdType.MESH
F32 = jnp.float32
BF16 = jnp.bfloat16

masked_fill = -1e30
gamma_floor = 0.01

TOK = 128
HEAD = 128
SPAN = 64
NZ = 8
FEAT = 256
COLS = 512
CHIPS = 16


def aligned(index, size):
    return pl.ds(pl.multiple_of(index * size, size), size)


def contract(left, right, left_dim, right_dim):
    return lax.dot_general(
        left, right, (((left_dim,), (right_dim,)), ((), ())), preferred_element_type=F32
    )


class Sent:
    def __init__(self, copy):
        self.copy = copy
        self.open_send = self.open_recv = True
        copy.start()

    def wait_recv(self):
        if self.open_recv:
            self.copy.wait_recv()
        self.open_recv = False

    def wait_send(self):
        if self.open_send:
            self.copy.wait_send()
        self.open_send = False


def kernel(
    scale_total,
    h_ref,
    q_ref,
    k_ref,
    v_ref,
    do_ref,
    span_ref,
    out_ref,
    hid,
    raw,
    keys,
    keys_t,
    values,
    queries,
    douts,
    expo,
    dprob,
    tops,
    key_acc,
    value_acc,
    query_acc,
    grads,
    acc,
    norm_box,
    norm_far,
    half_in,
    rs_out,
    rs_in,
    ag,
    spans,
    slots,
    hid_ss,
    hid_rs,
    ring_ss,
    ring_rs,
    twin_ss,
    twin_rs,
    fwd_ss,
    fwd_rs,
    norm_ss,
    norm_rs,
    rs_ss,
    rs_rs,
    ag_ss,
    ag_rs,
    own_sem,
    word,
):
    dp = lax.axis_index("dp")
    ctx = lax.axis_index("ctx")
    z = ctx // 2
    yl = lax.rem(ctx, 2)
    core = lax.rem(dp, 2)
    chip = dp // 2
    inv_scale = 1.0 / math.sqrt(HEAD)

    def zed(step):
        return lax.rem(z + step + NZ, NZ)

    up = (dp, zed(1) * 2 + yl)
    down = (dp, zed(-1) * 2 + yl)
    pair = (dp, z * 2 + (1 - yl))
    far_dp = chip * 2 + (1 - core)
    twin = (far_dp, ctx)

    def ctx_peer(step):
        return lax.rem(ctx + step, 16)

    def chip_peer(step):
        return lax.rem(chip // 4 + step // 4, 4) * 4 + lax.rem(chip + step % 4, 4)

    ctx_order = [8, 9, 7, 10, 6, 11, 5, 12, 4, 13, 3, 14, 2, 15, 1]
    started = []

    def send(src, dst, ss, rs, device):
        copy = Sent(
            pltpu.make_async_remote_copy(
                src_ref=src, dst_ref=dst, send_sem=ss, recv_sem=rs,
                device_id=device, device_id_type=MESH,
            )
        )
        started.append(copy)
        return copy

    def finish():
        for copy in started:
            copy.wait_recv()
            copy.wait_send()

    mine = aligned(ctx, TOK)
    loads = [pltpu.make_async_copy(span_ref, spans, own_sem.at[8])]
    for n, (ref, start, width) in enumerate(
        [(k_ref, 0, 128), (v_ref, 128, 128), (q_ref, 256, 256), (do_ref, 512, 256)]
    ):
        for s in range(2):
            loads.append(
                pltpu.make_async_copy(
                    ref.at[0, pl.ds(s * SPAN, SPAN)],
                    raw.at[2 * ctx + s, :, pl.ds(start, width)],
                    own_sem.at[2 * n + s],
                )
            )
    for load in loads:
        load.start()

    def signal(sem, *devices):
        for device in devices:
            pl.semaphore_signal(sem, inc=1, device_id=device, device_id_type=MESH)

    x_near = [(chip_peer(step) * 2 + core, ctx) for step in (1, 3)]
    y_near = [(chip_peer(step) * 2 + core, ctx) for step in (4, 12)]
    barrier = pltpu.get_barrier_semaphore()
    signal(barrier, up, down, pair, twin, *x_near, *y_near)
    for load in loads:
        load.wait()
    pl.semaphore_wait(barrier, 8)
    signal(word.at[0], *x_near)

    def ring_send(lane, step, view_up, view_down):
        return (
            send(view_up, view_up, ring_ss.at[lane, 0, step], ring_rs.at[lane, 0, step], up),
            send(view_down, view_down, ring_ss.at[lane, 1, step], ring_rs.at[lane, 1, step], down),
        )

    def forward(lane, place, block_z, columns):
        view = raw.at[pl.ds(block_z * 4 + yl * 2, 2), :, columns]
        return send(view, view, fwd_ss.at[lane, place], fwd_rs.at[lane, place], pair)

    forwards = []

    def z_first(lane, start, width):
        columns = pl.ds(start, width)

        def views(step):
            if step < 4:
                return (
                    raw.at[pl.ds(zed(1 - step) * 4 + yl * 2, 2), :, columns],
                    raw.at[pl.ds(zed(step - 1) * 4 + yl * 2, 2), :, columns],
                )
            return (
                raw.at[zed(-3) * 4 + yl * 2, :, columns],
                raw.at[zed(3) * 4 + yl * 2 + 1, :, columns],
            )

        copies = ring_send(lane, 1, *views(1))
        forwards.append(forward(lane, 0, z, columns))
        yield
        for step in range(1, 5):
            for copy in copies:
                copy.wait_recv()
            if step < 4:
                copies = ring_send(lane, step + 1, *views(step + 1))
                forwards.append(forward(lane, 2 * step - 1, zed(-step), columns))
                forwards.append(forward(lane, 2 * step, zed(step), columns))
            else:
                forwards.append(forward(lane, 7, zed(4), columns))
            yield

    def y_first(lane, start, width):
        columns = pl.ds(start, width)
        exchange = forward(lane, 0, z, columns)
        yield

        def views(step):
            if step < 4:
                return (
                    raw.at[pl.ds(zed(1 - step) * 4, 4), :, columns],
                    raw.at[pl.ds(zed(step - 1) * 4, 4), :, columns],
                )
            return (
                raw.at[pl.ds(zed(-3) * 4, 2), :, columns],
                raw.at[pl.ds(zed(3) * 4 + 2, 2), :, columns],
            )

        exchange.wait_recv()
        copies = ring_send(lane, 1, *views(1))
        yield
        for step in range(1, 5):
            for copy in copies:
                copy.wait_recv()
            if step < 4:
                copies = ring_send(lane, step + 1, *views(step + 1))
            yield

    lanes = [y_first(0, 0, 256), z_first(1, 256, 256), z_first(2, 512, 256)]
    for lane in lanes:
        next(lane)
    for lane in lanes[:1]:
        next(lane)

    own_copy = pltpu.make_async_copy(
        h_ref.at[0, :, aligned(ctx, FEAT)], hid.at[mine, :], own_sem.at[9]
    )
    own_copy.start()

    def find_slot(block, carry):
        slot = jnp.int32(0)
        for s in range(32):
            slot = jnp.where(spans[0, s] == block, jnp.int32(s), slot)
        slots[block] = slot
        return carry

    lax.fori_loop(0, 32, find_slot, 0)
    hid_copies = []

    def send_features(aheads):
        for ahead in aheads:
            peer = ctx_peer(ahead)
            hid_copies.append(
                send(
                    h_ref.at[0, :, aligned(peer, FEAT)], hid.at[mine, :],
                    hid_ss.at[ahead], hid_rs.at[ahead], (dp, peer),
                )
            )

    early = {3: [8], 4: [6, 10, 4, 12, 2, 14]}
    for step in range(1, 5):
        for lane in lanes:
            next(lane)
        send_features(early.get(step, []))
    for copy in forwards:
        copy.wait_recv()

    signal(word.at[3], twin)
    pl.semaphore_wait(word.at[0], 2)
    signal(word.at[1], *y_near)
    send_features([9, 7, 11, 5, 13, 3, 15, 1])

    def place_block(block, carry):
        rows = raw[slots[block]]
        keys[aligned(block, SPAN), :] = rows[:, :128]
        values[aligned(block, SPAN), :] = rows[:, 128:256]
        tile = block // 4
        for h in range(2):
            into = aligned(h * 4 + lax.rem(block, 4), SPAN)
            queries[tile, into, :] = rows[:, 256 + h * 128 : 384 + h * 128]
            douts[tile, into, :] = rows[:, 512 + h * 128 : 640 + h * 128]
        return carry

    lax.fori_loop(0, 32, place_block, 0)
    keys_t[...] = keys[...].T

    to_log2 = inv_scale * math.log2(math.e)

    def totals(tile, block, head, running):
        top, total, dot = running
        lanes = pl.ds(head * 256, 256)
        query, dout = queries[tile, lanes, :], douts[tile, lanes, :]
        for part in range(2):
            rows = pl.ds(block * 256 + part * 128, 128)
            scores = contract(keys[rows, :], query, 1, 1) * to_log2
            if block == tile:
                key_at = lax.broadcasted_iota(jnp.int32, (128, 256), 0) + part * 128
                query_at = lax.broadcasted_iota(jnp.int32, (128, 256), 1)
                scores = jnp.where(key_at <= query_at, scores, masked_fill)
            probs = contract(values[rows, :], dout, 1, 1)
            here = jnp.max(scores, axis=0, keepdims=True)
            weights = jnp.exp2(scores - here)
            expo[rows, lanes] = weights
            dprob[rows, lanes] = probs
            tops[block * 2 + part, :, lanes] = jnp.broadcast_to(here, (8, 256))
            new_top = jnp.maximum(top, here)
            old, new = jnp.exp2(top - new_top), jnp.exp2(here - new_top)
            total = old * total + new * jnp.sum(weights, axis=0, keepdims=True)
            dot = old * dot + new * jnp.sum(weights * probs, axis=0, keepdims=True)
            top = new_top
        return top, total, dot

    def gradients(tile, block, log_total, row_delta):
        probs = jnp.concatenate(
            [
                expo[pl.ds(block * 256 + part * 128, 128), :]
                * jnp.exp2(tops[block * 2 + part, 0:1, :] - log_total)
                for part in range(2)
            ],
            axis=0,
        )
        rows = pl.ds(block * 256, 256)
        scores_low = (probs * (dprob[rows, :] - row_delta)).astype(BF16)
        value_add = jnp.dot(probs.astype(BF16), douts[tile], preferred_element_type=F32)
        key_add = jnp.dot(scores_low, queries[tile], preferred_element_type=F32)
        if tile == block:
            value_acc[rows, :] = value_add
            key_acc[rows, :] = key_add
        else:
            value_acc[rows, :] += value_add
            key_acc[rows, :] += key_add
        return jnp.dot(keys_t[:, rows], scores_low, preferred_element_type=F32)

    for tile in range(8):
        heads = []
        for head in range(2):
            running = (
                jnp.full((1, 256), masked_fill, F32),
                jnp.zeros((1, 256), F32),
                jnp.zeros((1, 256), F32),
            )
            for block in [tile, *range(tile)]:
                running = totals(tile, block, head, running)
            heads.append(running)
        top, total, dot = (jnp.concatenate(both, axis=1) for both in zip(*heads))
        log_total = top + jnp.log2(total)
        row_delta = dot / total
        for block in range(tile + 1):
            query_add = gradients(tile, block, log_total, row_delta)
            if block == 0:
                query_acc[...] = query_add
            else:
                query_acc[...] += query_add
        query_sum = (query_acc[...].T * inv_scale).astype(BF16)
        rows = pl.ds(tile * 4, 4)
        grads[rows, :, :128] = query_sum[:256].reshape(4, SPAN, 128)
        grads[rows, :, 128:256] = query_sum[256:].reshape(4, SPAN, 128)

    grads[:, :, 256:384] = (key_acc[...] * inv_scale).astype(BF16).reshape(32, SPAN, 128)
    grads[:, :, 384:] = value_acc[...].astype(BF16).reshape(32, SPAN, 128)

    pl.semaphore_wait(word.at[1], 2)
    signal(word.at[2], *y_near)

    own_copy.wait()
    for copy in hid_copies:
        copy.wait_recv()

    for block in range(NZ):
        part = jnp.concatenate(
            [grads[spans[0, block * 4 + s]] for s in range(4)], axis=0
        )
        part = contract(hid[block * 256 : (block + 1) * 256, :], part, 0, 0)
        if block == 0:
            acc[...] = part
        else:
            acc[...] += part

    half_copy = send(
        acc.at[:, aligned(1 - core, FEAT)], half_in, twin_ss.at[0], twin_rs.at[0], twin
    )
    whole = acc[...]
    squares = jnp.sum((whole * whole).reshape(32, 8, COLS), axis=0)
    norm_box[ctx] = (
        squares[:, :128] + squares[:, 128:256] + squares[:, 256:384] + squares[:, 384:]
    )
    pl.semaphore_wait(word.at[3], 1)
    norm_copies = []
    for ahead in ctx_order + [0]:
        place = norm_box.at[ctx]
        if ahead:
            norm_copies.append(
                send(
                    place, place, norm_ss.at[0, ahead], norm_rs.at[0, ahead],
                    (dp, ctx_peer(ahead)),
                )
            )
        norm_copies.append(
            send(
                place, norm_far.at[ctx], norm_ss.at[1, ahead], norm_rs.at[1, ahead],
                (far_dp, ctx_peer(ahead)),
            )
        )
    for copy in norm_copies:
        copy.wait_recv()

    def factor_of(box):
        total_sq = jnp.sum(jnp.sum(box[...], axis=0), axis=(0, 1), keepdims=True)
        return scale_total / (jnp.sqrt(total_sq) + gamma_floor)

    near_factor = factor_of(norm_box)
    far_factor = factor_of(norm_far)
    half_copy.wait_recv()
    mixed = acc[:, aligned(core, FEAT)] * near_factor + half_in[...] * far_factor
    rs_out[...] = mixed.astype(BF16).reshape(CHIPS, 16, FEAT)

    chip_order = [10, 8, 2, 9, 11, 6, 14, 5, 7, 13, 15, 4, 12, 1, 3]
    pl.semaphore_wait(word.at[2], 2)
    rs_copies = []
    for step in chip_order:
        other = chip_peer(step)
        rs_copies.append(
            send(
                rs_out.at[other], rs_in.at[chip], rs_ss.at[step], rs_rs.at[step],
                (other * 2 + core, ctx),
            )
        )
    rs_in[chip] = rs_out[chip]
    for copy in rs_copies:
        copy.wait_recv()

    piece = rs_in[0].astype(F32)
    for place in range(1, CHIPS):
        piece += rs_in[place].astype(F32)
    ag[chip] = piece.astype(BF16)
    ag_copies = []
    for step in chip_order:
        other = chip_peer(step)
        ag_copies.append(
            send(
                ag.at[chip], ag.at[chip], ag_ss.at[step], ag_rs.at[step],
                (other * 2 + core, ctx),
            )
        )
    for copy in ag_copies:
        copy.wait_recv()

    half = out_ref.at[:, :, aligned(core, FEAT)]
    send(ag, half, twin_ss.at[1], twin_rs.at[1], twin)
    keep = pltpu.make_async_copy(ag, half, own_sem.at[10])
    keep.start()
    keep.wait()
    finish()


def on_device(hidden_in, query_states, key_states, value_states, out_grad, span_order):
    scale_total = math.sqrt(hidden_in.shape[2] * COLS / lax.axis_size("dp"))
    dma = pltpu.SemaphoreType.DMA
    summed = pl.pallas_call(
        functools.partial(kernel, scale_total),
        name="clipped_grads",
        out_shape=jax.ShapeDtypeStruct((CHIPS, 16, COLS), BF16),
        in_specs=[pl.BlockSpec(memory_space=pl.ANY)] * 6,
        out_specs=pl.BlockSpec(memory_space=pl.ANY),
        scratch_shapes=[
            pltpu.VMEM((16 * TOK, FEAT), BF16),
            pltpu.VMEM((32, SPAN, 6 * HEAD), BF16),
            pltpu.VMEM((16 * TOK, HEAD), BF16),
            pltpu.VMEM((HEAD, 16 * TOK), BF16),
            pltpu.VMEM((16 * TOK, HEAD), BF16),
            pltpu.VMEM((8, 512, HEAD), BF16),
            pltpu.VMEM((8, 512, HEAD), BF16),
            pltpu.VMEM((16 * TOK, 512), F32),
            pltpu.VMEM((16 * TOK, 512), F32),
            pltpu.VMEM((16, 8, 512), F32),
            pltpu.VMEM((16 * TOK, HEAD), F32),
            pltpu.VMEM((16 * TOK, HEAD), F32),
            pltpu.VMEM((HEAD, 512), F32),
            pltpu.VMEM((32, SPAN, COLS), BF16),
            pltpu.VMEM((FEAT, COLS), F32),
            pltpu.VMEM((16, 8, 128), F32),
            pltpu.VMEM((16, 8, 128), F32),
            pltpu.VMEM((FEAT, FEAT), F32),
            pltpu.VMEM((CHIPS, 16, FEAT), BF16),
            pltpu.VMEM((CHIPS, 16, FEAT), BF16),
            pltpu.VMEM((CHIPS, 16, FEAT), BF16),
            pltpu.SMEM((1, 32), jnp.int32),
            pltpu.SMEM((32,), jnp.int32),
            dma((16,)), dma((16,)),
            dma((6, 2, 5)), dma((6, 2, 5)),
            dma((2,)), dma((2,)),
            dma((6, 8)), dma((6, 8)),
            dma((2, 16)), dma((2, 16)),
            dma((16,)), dma((16,)),
            dma((16,)), dma((16,)),
            dma((11,)),
            pltpu.SemaphoreType.REGULAR((4,)),
        ],
        compiler_params=pltpu.CompilerParams(
            collective_id=0, has_side_effects=True, vmem_limit_bytes=62 << 20
        ),
    )(hidden_in, query_states, key_states, value_states, out_grad, span_order)
    return summed.astype(F32).reshape(FEAT, COLS)


def solution(mesh):
    return jax.shard_map(
        on_device,
        mesh=mesh,
        in_specs=(
            P("dp", "ctx", None),
            P("dp", "ctx", None),
            P("dp", "ctx", None),
            P("dp", "ctx", None),
            P("dp", "ctx", None),
            P("dp", None),
        ),
        out_specs=P("ctx", None),
        check_vma=False,
    )
```

```python
import functools
import math

import jax
import jax.numpy as jnp
from jax import lax
from jax.experimental import pallas as pl
from jax.experimental.pallas import tpu as pltpu
from jax.sharding import PartitionSpec as P

MESH = pl.DeviceIdType.MESH
F32 = jnp.float32
BF16 = jnp.bfloat16

masked_fill = -1e30
gamma_floor = 0.01

TOK = 128
HEAD = 128
SPAN = 64
NZ = 8
FEAT = 256
COLS = 512
CHIPS = 16


def aligned(index, size):
    return pl.ds(pl.multiple_of(index * size, size), size)


def contract(left, right, left_dim, right_dim):
    return lax.dot_general(
        left, right, (((left_dim,), (right_dim,)), ((), ())), preferred_element_type=F32
    )


class Sent:
    def __init__(self, copy):
        self.copy = copy
        self.open_send = self.open_recv = True
        copy.start()

    def wait_recv(self):
        if self.open_recv:
            self.copy.wait_recv()
        self.open_recv = False

    def wait_send(self):
        if self.open_send:
            self.copy.wait_send()
        self.open_send = False


def kernel(
    scale_total,
    h_ref,
    q_ref,
    k_ref,
    v_ref,
    do_ref,
    span_ref,
    out_ref,
    hid,
    raw,
    keys,
    keys_t,
    values,
    queries,
    douts,
    expo,
    dprob,
    tops,
    key_acc,
    value_acc,
    query_acc,
    grads,
    acc,
    norm_box,
    norm_far,
    half_in,
    rs_out,
    rs_in,
    ag,
    spans,
    slots,
    hid_ss,
    hid_rs,
    ring_ss,
    ring_rs,
    twin_ss,
    twin_rs,
    fwd_ss,
    fwd_rs,
    norm_ss,
    norm_rs,
    rs_ss,
    rs_rs,
    ag_ss,
    ag_rs,
    own_sem,
    word,
):
    dp = lax.axis_index("dp")
    ctx = lax.axis_index("ctx")
    z = ctx // 2
    yl = lax.rem(ctx, 2)
    core = lax.rem(dp, 2)
    chip = dp // 2
    inv_scale = 1.0 / math.sqrt(HEAD)

    def zed(step):
        return lax.rem(z + step + NZ, NZ)

    up = (dp, zed(1) * 2 + yl)
    down = (dp, zed(-1) * 2 + yl)
    pair = (dp, z * 2 + (1 - yl))
    far_dp = chip * 2 + (1 - core)
    twin = (far_dp, ctx)

    def ctx_peer(step):
        return lax.rem(ctx + step, 16)

    def chip_peer(step):
        return lax.rem(chip // 4 + step // 4, 4) * 4 + lax.rem(chip + step % 4, 4)

    ctx_order = [8, 9, 7, 10, 6, 11, 5, 12, 4, 13, 3, 14, 2, 15, 1]
    started = []

    def send(src, dst, ss, rs, device):
        copy = Sent(
            pltpu.make_async_remote_copy(
                src_ref=src, dst_ref=dst, send_sem=ss, recv_sem=rs,
                device_id=device, device_id_type=MESH,
            )
        )
        started.append(copy)
        return copy

    def finish():
        for copy in started:
            copy.wait_recv()
            copy.wait_send()

    mine = aligned(ctx, TOK)
    loads = [pltpu.make_async_copy(span_ref, spans, own_sem.at[8])]
    for n, (ref, start, width) in enumerate(
        [(k_ref, 0, 128), (v_ref, 128, 128), (q_ref, 256, 256), (do_ref, 512, 256)]
    ):
        for s in range(2):
            loads.append(
                pltpu.make_async_copy(
                    ref.at[0, pl.ds(s * SPAN, SPAN)],
                    raw.at[2 * ctx + s, :, pl.ds(start, width)],
                    own_sem.at[2 * n + s],
                )
            )
    for load in loads:
        load.start()

    def signal(sem, *devices):
        for device in devices:
            pl.semaphore_signal(sem, inc=1, device_id=device, device_id_type=MESH)

    x_near = [(chip_peer(step) * 2 + core, ctx) for step in (1, 3)]
    y_near = [(chip_peer(step) * 2 + core, ctx) for step in (4, 12)]
    barrier = pltpu.get_barrier_semaphore()
    signal(barrier, up, down, pair, twin, *x_near, *y_near)
    for load in loads:
        load.wait()
    pl.semaphore_wait(barrier, 8)
    signal(word.at[0], *x_near)

    def ring_send(lane, step, view_up, view_down):
        return (
            send(view_up, view_up, ring_ss.at[lane, 0, step], ring_rs.at[lane, 0, step], up),
            send(view_down, view_down, ring_ss.at[lane, 1, step], ring_rs.at[lane, 1, step], down),
        )

    def forward(lane, place, block_z, columns):
        view = raw.at[pl.ds(block_z * 4 + yl * 2, 2), :, columns]
        return send(view, view, fwd_ss.at[lane, place], fwd_rs.at[lane, place], pair)

    forwards = []

    def z_first(lane, start, width):
        columns = pl.ds(start, width)

        def views(step):
            if step < 4:
                return (
                    raw.at[pl.ds(zed(1 - step) * 4 + yl * 2, 2), :, columns],
                    raw.at[pl.ds(zed(step - 1) * 4 + yl * 2, 2), :, columns],
                )
            return (
                raw.at[zed(-3) * 4 + yl * 2, :, columns],
                raw.at[zed(3) * 4 + yl * 2 + 1, :, columns],
            )

        copies = ring_send(lane, 1, *views(1))
        forwards.append(forward(lane, 0, z, columns))
        yield
        for step in range(1, 5):
            for copy in copies:
                copy.wait_recv()
            if step < 4:
                copies = ring_send(lane, step + 1, *views(step + 1))
                forwards.append(forward(lane, 2 * step - 1, zed(-step), columns))
                forwards.append(forward(lane, 2 * step, zed(step), columns))
            else:
                forwards.append(forward(lane, 7, zed(4), columns))
            yield

    def y_first(lane, start, width):
        columns = pl.ds(start, width)
        exchange = forward(lane, 0, z, columns)
        yield

        def views(step):
            if step < 4:
                return (
                    raw.at[pl.ds(zed(1 - step) * 4, 4), :, columns],
                    raw.at[pl.ds(zed(step - 1) * 4, 4), :, columns],
                )
            return (
                raw.at[pl.ds(zed(-3) * 4, 2), :, columns],
                raw.at[pl.ds(zed(3) * 4 + 2, 2), :, columns],
            )

        exchange.wait_recv()
        copies = ring_send(lane, 1, *views(1))
        yield
        for step in range(1, 5):
            for copy in copies:
                copy.wait_recv()
            if step < 4:
                copies = ring_send(lane, step + 1, *views(step + 1))
            yield

    lanes = [y_first(0, 0, 256), z_first(1, 256, 256), z_first(2, 512, 256)]
    for lane in lanes:
        next(lane)
    for lane in lanes[:1]:
        next(lane)

    own_copy = pltpu.make_async_copy(
        h_ref.at[0, :, aligned(ctx, FEAT)], hid.at[mine, :], own_sem.at[9]
    )
    own_copy.start()

    def find_slot(block, carry):
        slot = jnp.int32(0)
        for s in range(32):
            slot = jnp.where(spans[0, s] == block, jnp.int32(s), slot)
        slots[block] = slot
        return carry

    lax.fori_loop(0, 32, find_slot, 0)
    hid_copies = []

    def send_features(aheads):
        for ahead in aheads:
            peer = ctx_peer(ahead)
            hid_copies.append(
                send(
                    h_ref.at[0, :, aligned(peer, FEAT)], hid.at[mine, :],
                    hid_ss.at[ahead], hid_rs.at[ahead], (dp, peer),
                )
            )

    early = {}
    for step in range(1, 5):
        for lane in lanes:
            next(lane)
        send_features(early.get(step, []))
    for copy in forwards:
        copy.wait_recv()

    signal(word.at[3], twin)
    pl.semaphore_wait(word.at[0], 2)
    signal(word.at[1], *y_near)
    send_features([8, 9, 7, 10, 6, 11, 5, 12, 4, 13, 3, 14, 2, 15, 1])

    def place_block(block, carry):
        rows = raw[slots[block]]
        keys[aligned(block, SPAN), :] = rows[:, :128]
        values[aligned(block, SPAN), :] = rows[:, 128:256]
        tile = block // 4
        for h in range(2):
            into = aligned(h * 4 + lax.rem(block, 4), SPAN)
            queries[tile, into, :] = rows[:, 256 + h * 128 : 384 + h * 128]
            douts[tile, into, :] = rows[:, 512 + h * 128 : 640 + h * 128]
        return carry

    lax.fori_loop(0, 32, place_block, 0)
    keys_t[...] = keys[...].T

    to_log2 = inv_scale * math.log2(math.e)

    def totals(tile, block, head, running):
        top, total, dot = running
        lanes = pl.ds(head * 256, 256)
        query, dout = queries[tile, lanes, :], douts[tile, lanes, :]
        for part in range(2):
            rows = pl.ds(block * 256 + part * 128, 128)
            scores = contract(keys[rows, :], query, 1, 1) * to_log2
            if block == tile:
                key_at = lax.broadcasted_iota(jnp.int32, (128, 256), 0) + part * 128
                query_at = lax.broadcasted_iota(jnp.int32, (128, 256), 1)
                scores = jnp.where(key_at <= query_at, scores, masked_fill)
            probs = contract(values[rows, :], dout, 1, 1)
            here = jnp.max(scores, axis=0, keepdims=True)
            weights = jnp.exp2(scores - here)
            expo[rows, lanes] = weights
            dprob[rows, lanes] = probs
            tops[block * 2 + part, :, lanes] = jnp.broadcast_to(here, (8, 256))
            new_top = jnp.maximum(top, here)
            old, new = jnp.exp2(top - new_top), jnp.exp2(here - new_top)
            total = old * total + new * jnp.sum(weights, axis=0, keepdims=True)
            dot = old * dot + new * jnp.sum(weights * probs, axis=0, keepdims=True)
            top = new_top
        return top, total, dot

    def gradients(tile, block, log_total, row_delta):
        probs = jnp.concatenate(
            [
                expo[pl.ds(block * 256 + part * 128, 128), :]
                * jnp.exp2(tops[block * 2 + part, 0:1, :] - log_total)
                for part in range(2)
            ],
            axis=0,
        )
        rows = pl.ds(block * 256, 256)
        scores_low = (probs * (dprob[rows, :] - row_delta)).astype(BF16)
        value_add = jnp.dot(probs.astype(BF16), douts[tile], preferred_element_type=F32)
        key_add = jnp.dot(scores_low, queries[tile], preferred_element_type=F32)
        if tile == block:
            value_acc[rows, :] = value_add
            key_acc[rows, :] = key_add
        else:
            value_acc[rows, :] += value_add
            key_acc[rows, :] += key_add
        return jnp.dot(keys_t[:, rows], scores_low, preferred_element_type=F32)

    for tile in range(8):
        heads = []
        for head in range(2):
            running = (
                jnp.full((1, 256), masked_fill, F32),
                jnp.zeros((1, 256), F32),
                jnp.zeros((1, 256), F32),
            )
            for block in [tile, *range(tile)]:
                running = totals(tile, block, head, running)
            heads.append(running)
        top, total, dot = (jnp.concatenate(both, axis=1) for both in zip(*heads))
        log_total = top + jnp.log2(total)
        row_delta = dot / total
        for block in range(tile + 1):
            query_add = gradients(tile, block, log_total, row_delta)
            if block == 0:
                query_acc[...] = query_add
            else:
                query_acc[...] += query_add
        query_sum = (query_acc[...].T * inv_scale).astype(BF16)
        rows = pl.ds(tile * 4, 4)
        grads[rows, :, :128] = query_sum[:256].reshape(4, SPAN, 128)
        grads[rows, :, 128:256] = query_sum[256:].reshape(4, SPAN, 128)

    grads[:, :, 256:384] = (key_acc[...] * inv_scale).astype(BF16).reshape(32, SPAN, 128)
    grads[:, :, 384:] = value_acc[...].astype(BF16).reshape(32, SPAN, 128)

    pl.semaphore_wait(word.at[1], 2)
    signal(word.at[2], *y_near)

    def wait_features(ahead):
        source = h_ref.at[0, :, mine_features]
        pltpu.make_async_remote_copy(
            src_ref=source, dst_ref=hid.at[mine, :],
            send_sem=hid_ss.at[ahead], recv_sem=hid_rs.at[ahead],
            device_id=pair, device_id_type=MESH,
        ).wait_recv()

    mine_features = aligned(ctx, FEAT)
    own_copy.wait()
    for n, shift in enumerate([4, 3, 5, 2, 6, 1, 7, 0]):
        if shift:
            for ahead in (2 * shift + yl, 2 * shift + yl - 1):
                wait_features(ahead)
        else:
            wait_features(15 - 14 * yl)
        block = zed(-shift)
        part = jnp.concatenate([grads[spans[0, block * 4 + s]] for s in range(4)], axis=0)
        part = contract(hid[aligned(block, 256), :], part, 0, 0)
        if n == 0:
            acc[...] = part
        else:
            acc[...] += part
    for copy in hid_copies:
        copy.open_recv = False

    half_copy = send(
        acc.at[:, aligned(1 - core, FEAT)], half_in, twin_ss.at[0], twin_rs.at[0], twin
    )
    whole = acc[...]
    squares = jnp.sum((whole * whole).reshape(32, 8, COLS), axis=0)
    norm_box[ctx] = (
        squares[:, :128] + squares[:, 128:256] + squares[:, 256:384] + squares[:, 384:]
    )
    pl.semaphore_wait(word.at[3], 1)
    norm_copies = []
    for ahead in ctx_order + [0]:
        place = norm_box.at[ctx]
        if ahead:
            norm_copies.append(
                send(
                    place, place, norm_ss.at[0, ahead], norm_rs.at[0, ahead],
                    (dp, ctx_peer(ahead)),
                )
            )
        norm_copies.append(
            send(
                place, norm_far.at[ctx], norm_ss.at[1, ahead], norm_rs.at[1, ahead],
                (far_dp, ctx_peer(ahead)),
            )
        )
    for copy in norm_copies:
        copy.wait_recv()

    def factor_of(box):
        total_sq = jnp.sum(jnp.sum(box[...], axis=0), axis=(0, 1), keepdims=True)
        return scale_total / (jnp.sqrt(total_sq) + gamma_floor)

    near_factor = factor_of(norm_box)
    far_factor = factor_of(norm_far)
    half_copy.wait_recv()
    mixed = acc[:, aligned(core, FEAT)] * near_factor + half_in[...] * far_factor
    rs_out[...] = mixed.astype(BF16).reshape(CHIPS, 16, FEAT)

    chip_order = [10, 8, 2, 9, 11, 6, 14, 5, 7, 13, 15, 4, 12, 1, 3]
    pl.semaphore_wait(word.at[2], 2)
    rs_copies = []
    for step in chip_order:
        other = chip_peer(step)
        rs_copies.append(
            send(
                rs_out.at[other], rs_in.at[chip], rs_ss.at[step], rs_rs.at[step],
                (other * 2 + core, ctx),
            )
        )
    rs_in[chip] = rs_out[chip]
    for copy in rs_copies:
        copy.wait_recv()

    piece = rs_in[0].astype(F32)
    for place in range(1, CHIPS):
        piece += rs_in[place].astype(F32)
    ag[chip] = piece.astype(BF16)
    ag_copies = []
    for step in chip_order:
        other = chip_peer(step)
        ag_copies.append(
            send(
                ag.at[chip], ag.at[chip], ag_ss.at[step], ag_rs.at[step],
                (other * 2 + core, ctx),
            )
        )
    for copy in ag_copies:
        copy.wait_recv()

    half = out_ref.at[:, :, aligned(core, FEAT)]
    send(ag, half, twin_ss.at[1], twin_rs.at[1], twin)
    keep = pltpu.make_async_copy(ag, half, own_sem.at[10])
    keep.start()
    keep.wait()
    finish()


def on_device(hidden_in, query_states, key_states, value_states, out_grad, span_order):
    scale_total = math.sqrt(hidden_in.shape[2] * COLS / lax.axis_size("dp"))
    dma = pltpu.SemaphoreType.DMA
    summed = pl.pallas_call(
        functools.partial(kernel, scale_total),
        name="clipped_grads",
        out_shape=jax.ShapeDtypeStruct((CHIPS, 16, COLS), BF16),
        in_specs=[pl.BlockSpec(memory_space=pl.ANY)] * 6,
        out_specs=pl.BlockSpec(memory_space=pl.ANY),
        scratch_shapes=[
            pltpu.VMEM((16 * TOK, FEAT), BF16),
            pltpu.VMEM((32, SPAN, 6 * HEAD), BF16),
            pltpu.VMEM((16 * TOK, HEAD), BF16),
            pltpu.VMEM((HEAD, 16 * TOK), BF16),
            pltpu.VMEM((16 * TOK, HEAD), BF16),
            pltpu.VMEM((8, 512, HEAD), BF16),
            pltpu.VMEM((8, 512, HEAD), BF16),
            pltpu.VMEM((16 * TOK, 512), F32),
            pltpu.VMEM((16 * TOK, 512), F32),
            pltpu.VMEM((16, 8, 512), F32),
            pltpu.VMEM((16 * TOK, HEAD), F32),
            pltpu.VMEM((16 * TOK, HEAD), F32),
            pltpu.VMEM((HEAD, 512), F32),
            pltpu.VMEM((32, SPAN, COLS), BF16),
            pltpu.VMEM((FEAT, COLS), F32),
            pltpu.VMEM((16, 8, 128), F32),
            pltpu.VMEM((16, 8, 128), F32),
            pltpu.VMEM((FEAT, FEAT), F32),
            pltpu.VMEM((CHIPS, 16, FEAT), BF16),
            pltpu.VMEM((CHIPS, 16, FEAT), BF16),
            pltpu.VMEM((CHIPS, 16, FEAT), BF16),
            pltpu.SMEM((1, 32), jnp.int32),
            pltpu.SMEM((32,), jnp.int32),
            dma((16,)), dma((16,)),
            dma((6, 2, 5)), dma((6, 2, 5)),
            dma((2,)), dma((2,)),
            dma((6, 8)), dma((6, 8)),
            dma((2, 16)), dma((2, 16)),
            dma((16,)), dma((16,)),
            dma((16,)), dma((16,)),
            dma((11,)),
            pltpu.SemaphoreType.REGULAR((4,)),
        ],
        compiler_params=pltpu.CompilerParams(
            collective_id=0, has_side_effects=True, vmem_limit_bytes=62 << 20
        ),
    )(hidden_in, query_states, key_states, value_states, out_grad, span_order)
    return summed.astype(F32).reshape(FEAT, COLS)


def solution(mesh):
    return jax.shard_map(
        on_device,
        mesh=mesh,
        in_specs=(
            P("dp", "ctx", None),
            P("dp", "ctx", None),
            P("dp", "ctx", None),
            P("dp", "ctx", None),
            P("dp", "ctx", None),
            P("dp", None),
        ),
        out_specs=P("ctx", None),
        check_vma=False,
    )
```

```python
import functools
import math

import jax
import jax.numpy as jnp
from jax import lax
from jax.experimental import pallas as pl
from jax.experimental.pallas import tpu as pltpu
from jax.sharding import PartitionSpec as P

MESH = pl.DeviceIdType.MESH
F32 = jnp.float32
BF16 = jnp.bfloat16

masked_fill = -1e30
gamma_floor = 0.01

TOK = 128
HEAD = 128
SPAN = 64
NZ = 8
FEAT = 256
COLS = 512
CHIPS = 16


def aligned(index, size):
    return pl.ds(pl.multiple_of(index * size, size), size)


def contract(left, right, left_dim, right_dim):
    return lax.dot_general(
        left, right, (((left_dim,), (right_dim,)), ((), ())), preferred_element_type=F32
    )


class Sent:
    def __init__(self, copy):
        self.copy = copy
        self.open_send = self.open_recv = True
        copy.start()

    def wait_recv(self):
        if self.open_recv:
            self.copy.wait_recv()
        self.open_recv = False

    def wait_send(self):
        if self.open_send:
            self.copy.wait_send()
        self.open_send = False


def kernel(
    scale_total,
    h_ref,
    q_ref,
    k_ref,
    v_ref,
    do_ref,
    span_ref,
    out_ref,
    hid,
    raw,
    keys,
    keys_t,
    values,
    queries,
    douts,
    expo,
    dprob,
    tops,
    key_acc,
    value_acc,
    query_acc,
    grads,
    acc,
    norm_box,
    norm_far,
    half_in,
    rs_out,
    rs_in,
    ag,
    spans,
    slots,
    hid_ss,
    hid_rs,
    ring_ss,
    ring_rs,
    twin_ss,
    twin_rs,
    fwd_ss,
    fwd_rs,
    norm_ss,
    norm_rs,
    rs_ss,
    rs_rs,
    ag_ss,
    ag_rs,
    own_sem,
    word,
):
    dp = lax.axis_index("dp")
    ctx = lax.axis_index("ctx")
    z = ctx // 2
    yl = lax.rem(ctx, 2)
    core = lax.rem(dp, 2)
    chip = dp // 2
    inv_scale = 1.0 / math.sqrt(HEAD)

    def zed(step):
        return lax.rem(z + step + NZ, NZ)

    up = (dp, zed(1) * 2 + yl)
    down = (dp, zed(-1) * 2 + yl)
    pair = (dp, z * 2 + (1 - yl))
    far_dp = chip * 2 + (1 - core)
    twin = (far_dp, ctx)

    def ctx_peer(step):
        return lax.rem(ctx + step, 16)

    def chip_peer(step):
        return lax.rem(chip // 4 + step // 4, 4) * 4 + lax.rem(chip + step % 4, 4)

    ctx_order = [8, 9, 7, 10, 6, 11, 5, 12, 4, 13, 3, 14, 2, 15, 1]
    started = []

    def send(src, dst, ss, rs, device):
        copy = Sent(
            pltpu.make_async_remote_copy(
                src_ref=src, dst_ref=dst, send_sem=ss, recv_sem=rs,
                device_id=device, device_id_type=MESH,
            )
        )
        started.append(copy)
        return copy

    def finish():
        for copy in started:
            copy.wait_recv()
            copy.wait_send()

    mine = aligned(ctx, TOK)
    loads = [pltpu.make_async_copy(span_ref, spans, own_sem.at[8])]
    for n, (ref, start, width) in enumerate(
        [(k_ref, 0, 128), (v_ref, 128, 128), (q_ref, 256, 256), (do_ref, 512, 256)]
    ):
        for s in range(2):
            loads.append(
                pltpu.make_async_copy(
                    ref.at[0, pl.ds(s * SPAN, SPAN)],
                    raw.at[2 * ctx + s, :, pl.ds(start, width)],
                    own_sem.at[2 * n + s],
                )
            )
    for load in loads:
        load.start()

    def signal(sem, *devices):
        for device in devices:
            pl.semaphore_signal(sem, inc=1, device_id=device, device_id_type=MESH)

    x_near = [(chip_peer(step) * 2 + core, ctx) for step in (1, 3)]
    y_near = [(chip_peer(step) * 2 + core, ctx) for step in (4, 12)]
    barrier = pltpu.get_barrier_semaphore()
    signal(barrier, up, down, pair, twin, *x_near, *y_near)
    for load in loads:
        load.wait()
    pl.semaphore_wait(barrier, 8)
    signal(word.at[0], *x_near)

    def ring_send(lane, step, view_up, view_down):
        return (
            send(view_up, view_up, ring_ss.at[lane, 0, step], ring_rs.at[lane, 0, step], up),
            send(view_down, view_down, ring_ss.at[lane, 1, step], ring_rs.at[lane, 1, step], down),
        )

    def forward(lane, place, block_z, columns):
        view = raw.at[pl.ds(block_z * 4 + yl * 2, 2), :, columns]
        return send(view, view, fwd_ss.at[lane, place], fwd_rs.at[lane, place], pair)

    forwards = []

    def z_first(lane, start, width):
        columns = pl.ds(start, width)

        def views(step):
            if step < 4:
                return (
                    raw.at[pl.ds(zed(1 - step) * 4 + yl * 2, 2), :, columns],
                    raw.at[pl.ds(zed(step - 1) * 4 + yl * 2, 2), :, columns],
                )
            return (
                raw.at[zed(-3) * 4 + yl * 2, :, columns],
                raw.at[zed(3) * 4 + yl * 2 + 1, :, columns],
            )

        copies = ring_send(lane, 1, *views(1))
        forwards.append(forward(lane, 0, z, columns))
        yield
        for step in range(1, 5):
            for copy in copies:
                copy.wait_recv()
            if step < 4:
                copies = ring_send(lane, step + 1, *views(step + 1))
                forwards.append(forward(lane, 2 * step - 1, zed(-step), columns))
                forwards.append(forward(lane, 2 * step, zed(step), columns))
            else:
                forwards.append(forward(lane, 7, zed(4), columns))
            yield

    def y_first(lane, start, width):
        columns = pl.ds(start, width)
        exchange = forward(lane, 0, z, columns)
        yield

        def views(step):
            if step < 4:
                return (
                    raw.at[pl.ds(zed(1 - step) * 4, 4), :, columns],
                    raw.at[pl.ds(zed(step - 1) * 4, 4), :, columns],
                )
            return (
                raw.at[pl.ds(zed(-3) * 4, 2), :, columns],
                raw.at[pl.ds(zed(3) * 4 + 2, 2), :, columns],
            )

        exchange.wait_recv()
        copies = ring_send(lane, 1, *views(1))
        yield
        for step in range(1, 5):
            for copy in copies:
                copy.wait_recv()
            if step < 4:
                copies = ring_send(lane, step + 1, *views(step + 1))
            yield

    lanes = [y_first(0, 0, 256), z_first(1, 256, 256), z_first(2, 512, 256)]
    for lane in lanes:
        next(lane)
    for lane in lanes[:1]:
        next(lane)

    own_copy = pltpu.make_async_copy(
        h_ref.at[0, :, aligned(ctx, FEAT)], hid.at[mine, :], own_sem.at[9]
    )
    own_copy.start()

    def find_slot(block, carry):
        slot = jnp.int32(0)
        for s in range(32):
            slot = jnp.where(spans[0, s] == block, jnp.int32(s), slot)
        slots[block] = slot
        return carry

    lax.fori_loop(0, 32, find_slot, 0)
    hid_copies = []

    def send_features(aheads):
        for ahead in aheads:
            peer = ctx_peer(ahead)
            hid_copies.append(
                send(
                    h_ref.at[0, :, aligned(peer, FEAT)], hid.at[mine, :],
                    hid_ss.at[ahead], hid_rs.at[ahead], (dp, peer),
                )
            )

    early = {4: [8, 6, 10]}
    for step in range(1, 5):
        for lane in lanes:
            next(lane)
        send_features(early.get(step, []))
    for copy in forwards:
        copy.wait_recv()

    signal(word.at[3], twin)
    pl.semaphore_wait(word.at[0], 2)
    signal(word.at[1], *y_near)
    send_features([9, 7, 11, 5, 12, 4, 13, 3, 14, 2, 15, 1])

    def place_block(block, carry):
        rows = raw[slots[block]]
        keys[aligned(block, SPAN), :] = rows[:, :128]
        values[aligned(block, SPAN), :] = rows[:, 128:256]
        tile = block // 4
        for h in range(2):
            into = aligned(h * 4 + lax.rem(block, 4), SPAN)
            queries[tile, into, :] = rows[:, 256 + h * 128 : 384 + h * 128]
            douts[tile, into, :] = rows[:, 512 + h * 128 : 640 + h * 128]
        return carry

    lax.fori_loop(0, 32, place_block, 0)
    keys_t[...] = keys[...].T

    to_log2 = inv_scale * math.log2(math.e)

    def totals(tile, block, head, running):
        top, total, dot = running
        lanes = pl.ds(head * 256, 256)
        query, dout = queries[tile, lanes, :], douts[tile, lanes, :]
        for part in range(2):
            rows = pl.ds(block * 256 + part * 128, 128)
            scores = contract(keys[rows, :], query, 1, 1) * to_log2
            if block == tile:
                key_at = lax.broadcasted_iota(jnp.int32, (128, 256), 0) + part * 128
                query_at = lax.broadcasted_iota(jnp.int32, (128, 256), 1)
                scores = jnp.where(key_at <= query_at, scores, masked_fill)
            probs = contract(values[rows, :], dout, 1, 1)
            here = jnp.max(scores, axis=0, keepdims=True)
            weights = jnp.exp2(scores - here)
            expo[rows, lanes] = weights
            dprob[rows, lanes] = probs
            tops[block * 2 + part, :, lanes] = jnp.broadcast_to(here, (8, 256))
            new_top = jnp.maximum(top, here)
            old, new = jnp.exp2(top - new_top), jnp.exp2(here - new_top)
            total = old * total + new * jnp.sum(weights, axis=0, keepdims=True)
            dot = old * dot + new * jnp.sum(weights * probs, axis=0, keepdims=True)
            top = new_top
        return top, total, dot

    def gradients(tile, block, log_total, row_delta):
        probs = jnp.concatenate(
            [
                expo[pl.ds(block * 256 + part * 128, 128), :]
                * jnp.exp2(tops[block * 2 + part, 0:1, :] - log_total)
                for part in range(2)
            ],
            axis=0,
        )
        rows = pl.ds(block * 256, 256)
        scores_low = (probs * (dprob[rows, :] - row_delta)).astype(BF16)
        value_add = jnp.dot(probs.astype(BF16), douts[tile], preferred_element_type=F32)
        key_add = jnp.dot(scores_low, queries[tile], preferred_element_type=F32)
        if tile == block:
            value_acc[rows, :] = value_add
            key_acc[rows, :] = key_add
        else:
            value_acc[rows, :] += value_add
            key_acc[rows, :] += key_add
        return jnp.dot(keys_t[:, rows], scores_low, preferred_element_type=F32)

    for tile in range(8):
        heads = []
        for head in range(2):
            running = (
                jnp.full((1, 256), masked_fill, F32),
                jnp.zeros((1, 256), F32),
                jnp.zeros((1, 256), F32),
            )
            for block in [tile, *range(tile)]:
                running = totals(tile, block, head, running)
            heads.append(running)
        top, total, dot = (jnp.concatenate(both, axis=1) for both in zip(*heads))
        log_total = top + jnp.log2(total)
        row_delta = dot / total
        for block in range(tile + 1):
            query_add = gradients(tile, block, log_total, row_delta)
            if block == 0:
                query_acc[...] = query_add
            else:
                query_acc[...] += query_add
        query_sum = (query_acc[...].T * inv_scale).astype(BF16)
        rows = pl.ds(tile * 4, 4)
        grads[rows, :, :128] = query_sum[:256].reshape(4, SPAN, 128)
        grads[rows, :, 128:256] = query_sum[256:].reshape(4, SPAN, 128)

    grads[:, :, 256:384] = (key_acc[...] * inv_scale).astype(BF16).reshape(32, SPAN, 128)
    grads[:, :, 384:] = value_acc[...].astype(BF16).reshape(32, SPAN, 128)

    pl.semaphore_wait(word.at[1], 2)
    signal(word.at[2], *y_near)

    def wait_features(ahead):
        source = h_ref.at[0, :, mine_features]
        pltpu.make_async_remote_copy(
            src_ref=source, dst_ref=hid.at[mine, :],
            send_sem=hid_ss.at[ahead], recv_sem=hid_rs.at[ahead],
            device_id=pair, device_id_type=MESH,
        ).wait_recv()

    mine_features = aligned(ctx, FEAT)
    own_copy.wait()
    for n, shift in enumerate([4, 3, 5, 2, 6, 1, 7, 0]):
        if shift:
            for ahead in (2 * shift + yl, 2 * shift + yl - 1):
                wait_features(ahead)
        else:
            wait_features(15 - 14 * yl)
        block = zed(-shift)
        part = jnp.concatenate([grads[spans[0, block * 4 + s]] for s in range(4)], axis=0)
        part = contract(hid[aligned(block, 256), :], part, 0, 0)
        if n == 0:
            acc[...] = part
        else:
            acc[...] += part
    for copy in hid_copies:
        copy.open_recv = False

    half_copy = send(
        acc.at[:, aligned(1 - core, FEAT)], half_in, twin_ss.at[0], twin_rs.at[0], twin
    )
    whole = acc[...]
    squares = jnp.sum((whole * whole).reshape(32, 8, COLS), axis=0)
    norm_box[ctx] = (
        squares[:, :128] + squares[:, 128:256] + squares[:, 256:384] + squares[:, 384:]
    )
    pl.semaphore_wait(word.at[3], 1)
    norm_copies = []
    for ahead in ctx_order + [0]:
        place = norm_box.at[ctx]
        if ahead:
            norm_copies.append(
                send(
                    place, place, norm_ss.at[0, ahead], norm_rs.at[0, ahead],
                    (dp, ctx_peer(ahead)),
                )
            )
        norm_copies.append(
            send(
                place, norm_far.at[ctx], norm_ss.at[1, ahead], norm_rs.at[1, ahead],
                (far_dp, ctx_peer(ahead)),
            )
        )
    for copy in norm_copies:
        copy.wait_recv()

    def factor_of(box):
        total_sq = jnp.sum(jnp.sum(box[...], axis=0), axis=(0, 1), keepdims=True)
        return scale_total / (jnp.sqrt(total_sq) + gamma_floor)

    near_factor = factor_of(norm_box)
    far_factor = factor_of(norm_far)
    half_copy.wait_recv()
    mixed = acc[:, aligned(core, FEAT)] * near_factor + half_in[...] * far_factor
    rs_out[...] = mixed.astype(BF16).reshape(CHIPS, 16, FEAT)

    chip_order = [10, 8, 2, 9, 11, 6, 14, 5, 7, 13, 15, 4, 12, 1, 3]
    pl.semaphore_wait(word.at[2], 2)
    rs_copies = []
    for step in chip_order:
        other = chip_peer(step)
        rs_copies.append(
            send(
                rs_out.at[other], rs_in.at[chip], rs_ss.at[step], rs_rs.at[step],
                (other * 2 + core, ctx),
            )
        )
    rs_in[chip] = rs_out[chip]
    for copy in rs_copies:
        copy.wait_recv()

    piece = rs_in[0].astype(F32)
    for place in range(1, CHIPS):
        piece += rs_in[place].astype(F32)
    ag[chip] = piece.astype(BF16)
    ag_copies = []
    for step in chip_order:
        other = chip_peer(step)
        ag_copies.append(
            send(
                ag.at[chip], ag.at[chip], ag_ss.at[step], ag_rs.at[step],
                (other * 2 + core, ctx),
            )
        )
    for copy in ag_copies:
        copy.wait_recv()

    half = out_ref.at[:, :, aligned(core, FEAT)]
    send(ag, half, twin_ss.at[1], twin_rs.at[1], twin)
    keep = pltpu.make_async_copy(ag, half, own_sem.at[10])
    keep.start()
    keep.wait()
    finish()


def on_device(hidden_in, query_states, key_states, value_states, out_grad, span_order):
    scale_total = math.sqrt(hidden_in.shape[2] * COLS / lax.axis_size("dp"))
    dma = pltpu.SemaphoreType.DMA
    summed = pl.pallas_call(
        functools.partial(kernel, scale_total),
        name="clipped_grads",
        out_shape=jax.ShapeDtypeStruct((CHIPS, 16, COLS), BF16),
        in_specs=[pl.BlockSpec(memory_space=pl.ANY)] * 6,
        out_specs=pl.BlockSpec(memory_space=pl.ANY),
        scratch_shapes=[
            pltpu.VMEM((16 * TOK, FEAT), BF16),
            pltpu.VMEM((32, SPAN, 6 * HEAD), BF16),
            pltpu.VMEM((16 * TOK, HEAD), BF16),
            pltpu.VMEM((HEAD, 16 * TOK), BF16),
            pltpu.VMEM((16 * TOK, HEAD), BF16),
            pltpu.VMEM((8, 512, HEAD), BF16),
            pltpu.VMEM((8, 512, HEAD), BF16),
            pltpu.VMEM((16 * TOK, 512), F32),
            pltpu.VMEM((16 * TOK, 512), F32),
            pltpu.VMEM((16, 8, 512), F32),
            pltpu.VMEM((16 * TOK, HEAD), F32),
            pltpu.VMEM((16 * TOK, HEAD), F32),
            pltpu.VMEM((HEAD, 512), F32),
            pltpu.VMEM((32, SPAN, COLS), BF16),
            pltpu.VMEM((FEAT, COLS), F32),
            pltpu.VMEM((16, 8, 128), F32),
            pltpu.VMEM((16, 8, 128), F32),
            pltpu.VMEM((FEAT, FEAT), F32),
            pltpu.VMEM((CHIPS, 16, FEAT), BF16),
            pltpu.VMEM((CHIPS, 16, FEAT), BF16),
            pltpu.VMEM((CHIPS, 16, FEAT), BF16),
            pltpu.SMEM((1, 32), jnp.int32),
            pltpu.SMEM((32,), jnp.int32),
            dma((16,)), dma((16,)),
            dma((6, 2, 5)), dma((6, 2, 5)),
            dma((2,)), dma((2,)),
            dma((6, 8)), dma((6, 8)),
            dma((2, 16)), dma((2, 16)),
            dma((16,)), dma((16,)),
            dma((16,)), dma((16,)),
            dma((11,)),
            pltpu.SemaphoreType.REGULAR((4,)),
        ],
        compiler_params=pltpu.CompilerParams(
            collective_id=0, has_side_effects=True, vmem_limit_bytes=62 << 20
        ),
    )(hidden_in, query_states, key_states, value_states, out_grad, span_order)
    return summed.astype(F32).reshape(FEAT, COLS)


def solution(mesh):
    return jax.shard_map(
        on_device,
        mesh=mesh,
        in_specs=(
            P("dp", "ctx", None),
            P("dp", "ctx", None),
            P("dp", "ctx", None),
            P("dp", "ctx", None),
            P("dp", "ctx", None),
            P("dp", None),
        ),
        out_specs=P("ctx", None),
        check_vma=False,
    )
```
